256 devices in a mesh: dom: 16 (over x, y_lo, core), shell: 16 (over y_hi, z).
Axes of the slice: x: 4, y: 4 (y_hi: 2, y_lo: 2; y = y_hi * 2 + y_lo), z: 8, core: 2. Of those that a mesh axis runs over, the one named last changes fastest.
Arguments:
- particles: bfloat16 [2, 2048, 8192], P(None, 'dom', 'shell'), may hold values from -6 to 6
- references: bfloat16 [256, 2, 8192], P('dom', None, 'shell'), may hold values from -0.29882812 to 0.29882812
- trans_index: int32 [2048], P('dom'), may hold values from 0 to 48
- shell_map: int32 [8192], P('shell'), may hold values from 0 to 63, as said below
- rot_index: int32 [36, 8192], P(None, 'shell'), may hold values from 0 to 8191, as said below
- inv_sigma: float32 [64], replicated, may hold values from 0.3 to 3
Outputs:
- new_refs: float32 [256, 2, 8192], P('dom', None, 'shell')
The draws below stay inside these ranges and needn't reach their ends.
Inputs may be any that keep to these rules, and one draw needn't show every extreme that they name: `shell_map`: pixels f of block b = f // 512 have shells b * 4 to b * 4 + 3, each used in every block. For each rotation, rot_index restricted to each block of 512 pixels is a permutation of that block.
All inputs are finite; a program needn't handle non-finite values.
Results may differ from the reference program's by a relative error of at most 0.005.
Values may be sent and summed in bfloat16 or wider, within the bound.
No kernel may reach another device: no remote copies, remote signals or barrier semaphores. Data moves between devices by JAX's collectives and lax.ppermute only.
A program may use at most 128 MiB of HBM per device.

```python
import math
import jax
import jax.numpy as jnp
from jax import lax

CLASSES = 256
ROTS = 36
FREQ_DEV = 512
SH_DEV = 4
FREQ = 8192
SHELLS = 64
PARTICLES = 2048


def draw_shell_map(key, part):
    key = jax.random.fold_in(key, 11)
    blocks = FREQ // FREQ_DEV
    inner = jax.random.randint(key, (blocks, FREQ_DEV), 0, SH_DEV)
    pos = jnp.arange(FREQ_DEV, dtype=jnp.int32)
    inner = jnp.where(pos[None, :] < SH_DEV, pos[None, :] % SH_DEV, inner)
    base = jnp.arange(blocks, dtype=jnp.int32)[:, None] * SH_DEV
    return (inner + base).reshape(FREQ).astype(jnp.int32)


def draw_rot_index(key, part):
    key = jax.random.fold_in(key, 23)
    blocks = FREQ // FREQ_DEV
    rand = jax.random.randint(key, (ROTS, blocks, FREQ_DEV), 0, 1048576)
    pos = jnp.arange(FREQ_DEV, dtype=jnp.int32)
    order = jnp.argsort(rand * FREQ_DEV + pos[None, None, :], axis=2, stable=True).astype(jnp.int32)
    base = jnp.arange(blocks, dtype=jnp.int32)[None, :, None] * FREQ_DEV
    return (order + base).reshape(ROTS, FREQ).astype(jnp.int32)


def set_ends(values, stream_key, smallest, top_value):
    extent = values.shape
    spot = [jax.random.randint(jax.random.fold_in(stream_key, axis), (), 0, extent[axis]) for axis in range(len(extent))]
    values = values.at[tuple(spot)].set(smallest)
    longest = extent.index(max(extent))
    spot[longest] = (spot[longest] + 1) % extent[longest]
    return values.at[tuple(spot)].set(top_value)


def levels(own_key, dims, split, low, largest):
    level = 1.0
    for axis_at, blocks in split:
        draws = jax.random.uniform(jax.random.fold_in(jax.random.fold_in(own_key, 6), axis_at), (blocks,), jnp.float32, low / len(split), largest / len(split))
        level = level * jnp.repeat(jnp.exp(draws), dims[axis_at] // blocks).reshape((-1,) + (1,) * (len(dims) - 1 - axis_at))
    return level


def bell_draw(key, extent, deviation, limit, shards=(), kind=jnp.bfloat16):
    entries = deviation * jax.random.normal(key, extent, jnp.float32)
    if shards:
        entries = entries * levels(key, extent, shards, -0.22, 0.18)
    return jnp.clip(entries, -limit, limit).astype(kind)


def setup_inputs(seed: int = 0) -> dict:
    seeds = jax.random.split(jax.random.key(seed), 7)
    particles = bell_draw(seeds[0], (2, PARTICLES, FREQ), 1.0, 6.0, ((1, 16), (2, 16)))
    references = bell_draw(seeds[1], (CLASSES, 2, FREQ), 0.05, 0.29882812, ((0, 16), (2, 16)))
    trans_index = set_ends(jax.random.randint(seeds[2], (PARTICLES,), 0, 49), jax.random.fold_in(seeds[2], 1), 0, 48).astype(jnp.int32)
    shell_map = draw_shell_map(jax.random.fold_in(seeds[6], 71), 0)
    rot_index = draw_rot_index(jax.random.fold_in(seeds[6], 71), 0)
    inv_sigma = jnp.clip(jnp.exp(jax.random.uniform(seeds[5], (SHELLS,), jnp.float32, math.log(0.3), math.log(3.0))), 0.3, 3.0)
    return {"particles": particles, "references": references, "trans_index": trans_index, "shell_map": shell_map, "rot_index": rot_index, "inv_sigma": inv_sigma}


def shift_images(particles, trans_index, fidx):
    kx = (fidx % 64).astype(jnp.float32)
    ky = ((fidx // 64) % 128 - 64).astype(jnp.float32)
    tx = (trans_index % 7 - 3).astype(jnp.float32)
    ty = (trans_index // 7 - 3).astype(jnp.float32)
    phase = (2.0 * jnp.pi / 128.0) * (tx[:, None] * kx[None, :] + ty[:, None] * ky[None, :])
    cosine = jnp.cos(phase)
    sine = jnp.sin(phase)
    real_part = particles[0].astype(jnp.float32)
    imag_part = particles[1].astype(jnp.float32)
    return jnp.stack([real_part * cosine + imag_part * sine, imag_part * cosine - real_part * sine])


def reference(particles, references, trans_index, shell_map, rot_index, inv_sigma):
    fidx = jnp.arange(FREQ, dtype=jnp.int32)
    moved = shift_images(particles, trans_index, fidx).astype(jnp.bfloat16)
    gain = inv_sigma[shell_map]
    weighted = (moved.astype(jnp.float32) * gain[None, None, :]).astype(jnp.bfloat16)
    weighted_f = weighted.astype(jnp.float32)

    def one_class(ref_k):
        rotated = ref_k[:, rot_index].astype(jnp.float32)
        cross = jnp.einsum('cnf,crf->nr', weighted_f, rotated)
        norm = jnp.einsum('crf,f->r', rotated * rotated, gain)
        return cross - 0.5 * norm[None, :]

    scores = jnp.transpose(lax.map(one_class, references), (1, 0, 2))
    flat = scores.reshape(scores.shape[0], -1)
    peak = jnp.max(flat, axis=1, keepdims=True)
    expo = jnp.exp(flat - peak)
    weights = (expo / jnp.sum(expo, axis=1, keepdims=True)).astype(jnp.bfloat16)
    weights = weights.reshape(scores.shape)
    inverse = jnp.zeros((ROTS, FREQ), jnp.int32).at[jnp.arange(ROTS, dtype=jnp.int32)[:, None], rot_index].set(fidx[None, :])

    def add_rotation(acc, step):
        w_r = weights[:, :, step].astype(jnp.float32)
        back = moved[:, :, inverse[step]].astype(jnp.float32)
        return acc + jnp.einsum('nk,cng->kcg', w_r, back), None

    sums, _ = lax.scan(add_rotation, jnp.zeros((CLASSES, 2, FREQ), jnp.float32), jnp.arange(ROTS, dtype=jnp.int32))
    totals = jnp.sum(weights.astype(jnp.float32), axis=(0, 2))
    return sums / (totals + 1.0)[:, None, None]
```

```python
import jax
import jax.numpy as jnp
import numpy as np
from jax import lax
from jax.experimental import pallas as pl
from jax.experimental.pallas import tpu as pltpu
from jax.sharding import Mesh, PartitionSpec as P

F32, F16, BF16 = jnp.float32, jnp.float16, jnp.bfloat16


def shift_images(particles, trans_index, fidx):
    kx = (fidx % 64).astype(F32)
    ky = (fidx // 64 % 128 - 64).astype(F32)
    tx = (trans_index % 7 - 3).astype(F32)
    ty = (trans_index // 7 - 3).astype(F32)
    phase = 2.0 * jnp.pi / 128.0 * (tx[:, None] * kx[None, :] + ty[:, None] * ky[None, :])
    cosine = jnp.cos(phase)
    sine = jnp.sin(phase)
    real_part = particles[0].astype(F32)
    imag_part = particles[1].astype(F32)
    return jnp.stack([real_part * cosine + imag_part * sine, imag_part * cosine - real_part * sine])


def unrotate_kernel(block, rows_ref, rot_ref, unrot_ref, weighted_ref, gain_ref):
    parts = unrot_ref.shape[1]
    place = lax.broadcasted_iota(jnp.int32, (block, block), 0)
    for b in range(rows_ref.shape[1] // block):
        at = slice(b * block, (b + 1) * block)
        hit = place == rot_ref[0, :, at]
        table = jnp.where(hit, 1.0, 0.0).astype(BF16)
        turned = lax.dot_general(
            rows_ref[:, at], table, (((1,), (1,)), ((), ())), preferred_element_type=F32
        )
        gain = jnp.sum(turned[2 * parts :], axis=0, keepdims=True)
        gain_ref[0, :, at] = gain
        unrot = turned[: 2 * parts]
        scaled = unrot * gain
        for c in range(2):
            unrot_ref[c, :, at] = unrot[c * parts : (c + 1) * parts].astype(BF16)
            weighted_ref[c, :, at] = scaled[c * parts : (c + 1) * parts].astype(BF16)


def unrotate(rows, rot, parts, block):
    rots, pixels = rot.shape
    spec = pl.BlockSpec((2, parts, pixels), lambda r: (0, r, 0))
    return pl.pallas_call(
        lambda *refs: unrotate_kernel(block, *refs),
        grid=(rots,),
        in_specs=[
            pl.BlockSpec(rows.shape, lambda r: (0, 0)),
            pl.BlockSpec((1, 1, pixels), lambda r: (r, 0, 0)),
        ],
        out_specs=[spec, spec, pl.BlockSpec((1, 1, pixels), lambda r: (r, 0, 0))],
        out_shape=[
            jax.ShapeDtypeStruct((2, rots * parts, pixels), BF16),
            jax.ShapeDtypeStruct((2, rots * parts, pixels), BF16),
            jax.ShapeDtypeStruct((rots, 1, pixels), F32),
        ],
        compiler_params=pltpu.CompilerParams(vmem_limit_bytes=32 * 1024 * 1024),
    )(rows, rot[:, None, :])


def shards(particles, references, trans_index, shell_map, rot_index, inv_sigma):
    _, parts, freq = particles.shape
    k_dev = references.shape[0]
    rots = rot_index.shape[0]
    shells = inv_sigma.shape[0]
    doms, zs = lax.axis_size("dom"), lax.axis_size("z")
    half = parts // 2
    eight = half // zs
    classes = doms * k_dev
    yh, z = lax.axis_index("yh"), lax.axis_index("z")
    first = yh == 0

    local_rot = rot_index - (yh * zs + z) * freq
    side = jnp.concatenate(
        [
            (local_rot >> 8).astype(BF16),
            (local_rot & 255).astype(BF16),
            shell_map[None].astype(BF16),
            jnp.zeros((7, freq), BF16),
        ]
    )
    give = lax.dynamic_slice_in_dim(particles, (1 - yh) * half, half, 1).reshape(2 * half, freq)
    keep = lax.dynamic_slice_in_dim(particles, yh * half, half, 1).reshape(2 * half, freq)
    got = lax.ppermute(jnp.concatenate([give, side]), "yh", [(0, 1), (1, 0)])
    own = jnp.concatenate([keep, side])
    both = jnp.concatenate([jnp.where(first, own, got), jnp.where(first, got, own)], axis=1)

    mine = references.transpose(1, 0, 2).reshape(1, 2 * k_dev, freq)
    pieces = lax.all_to_all(jnp.broadcast_to(mine, (2 * doms, 2 * k_dev, freq)), ("dom", "yh"), 0, 0)
    refs = pieces.reshape(doms, 2, 2, k_dev, freq).transpose(2, 0, 3, 1, 4).reshape(2, classes, 2 * freq)

    pos = jnp.arange(freq, dtype=jnp.int32)
    fidx = jnp.concatenate([z * freq + pos, (zs + z) * freq + pos])
    trans = lax.dynamic_slice_in_dim(trans_index, yh * half, half, 0)
    moved = shift_images(both[: 2 * half].reshape(2, half, 2 * freq), trans, fidx).astype(BF16)
    info = both[2 * half :].astype(F32)
    rot = (info[:rots] * 256.0 + info[rots : 2 * rots]).astype(jnp.int32)
    select = info[2 * rots][:, None] == jnp.arange(shells, dtype=F32)[None, :]
    gain = jnp.sum(jnp.where(select, inv_sigma[None, :], 0.0), axis=1)
    top = lax.reduce_precision(gain, 8, 7)
    middle = lax.reduce_precision(gain - top, 8, 7)
    low = gain - top - middle
    rows = jnp.concatenate(
        [moved.reshape(2 * half, 2 * freq), jnp.stack([top, middle, low]).astype(BF16), jnp.zeros((13, 2 * freq), BF16)]
    )
    unrot, weighted, gain_unrot = unrotate(rows, rot, half, freq)

    cross = jnp.einsum("cmg,ckg->mk", weighted, refs, preferred_element_type=F32)
    refs_f = refs.astype(F32)
    power = jnp.sum(refs_f * refs_f, axis=0)
    norm = jnp.einsum("rg,kg->rk", gain_unrot[:, 0], power, precision=lax.Precision.HIGHEST)
    partial = cross.reshape(rots, zs, eight, classes) - 0.5 * norm[:, None, None, :]
    partial = partial.transpose(1, 0, 2, 3).astype(F16).reshape(zs, rots * eight, classes)
    scores = jnp.sum(lax.all_to_all(partial, "z", 0, 0).astype(F32), axis=0).reshape(rots, eight, classes)
    peak = jnp.max(scores, axis=(0, 2), keepdims=True)
    expo = jnp.exp(scores - peak)
    weights = (expo / jnp.sum(expo, axis=(0, 2), keepdims=True)).astype(BF16)
    spread = jnp.broadcast_to(weights.reshape(1, rots * eight, classes), (zs, rots * eight, classes))
    weights = lax.all_to_all(spread, "z", 0, 0).reshape(zs, rots, eight, classes).transpose(1, 0, 2, 3)
    weights = weights.reshape(rots * half, classes)

    terms = jnp.einsum("mk,cmg->ckg", weights, unrot, preferred_element_type=F32)
    totals = jnp.sum(weights.astype(F32), axis=0).reshape(doms, 1, k_dev, 1)
    high = totals.astype(F16)
    rest = (totals - high.astype(F32)).astype(F16)
    tail = jnp.concatenate([high, rest, jnp.zeros((doms, 1, k_dev, 126), F16)], axis=3)
    terms = terms.reshape(2, doms, k_dev, 2, freq).transpose(1, 3, 2, 0, 4).reshape(doms, 2, k_dev, 2 * freq)
    message = jnp.concatenate([terms.astype(F16), jnp.broadcast_to(tail, (doms, 2, k_dev, 128))], axis=3)
    message = lax.all_to_all(message.reshape(2 * doms, k_dev, 2 * freq + 128), ("dom", "yh"), 0, 0)
    summed = jnp.sum(message.astype(F32), axis=0)
    counts = summed[:, 2 * freq] + summed[:, 2 * freq + 1]
    return (summed[:, : 2 * freq] / (counts + 1.0)[:, None]).reshape(k_dev, 2, freq)


def solution(mesh):
    doms, others = mesh.devices.shape
    grid = Mesh(mesh.devices.reshape(doms, 2, others // 2), ("dom", "yh", "z"))
    across = ("yh", "z")
    return jax.shard_map(
        shards,
        mesh=grid,
        in_specs=(
            P(None, "dom", across),
            P("dom", None, across),
            P("dom"),
            P(across),
            P(None, across),
            P(),
        ),
        out_specs=P("dom", None, across),
        check_vma=False,
    )
```

```python
import functools
import jax
import jax.numpy as jnp
from jax import lax
from jax.experimental import pallas as pl
from jax.experimental.pallas import tpu as pltpu
from jax.sharding import Mesh, PartitionSpec as P

F32, F16, BF16 = jnp.float32, jnp.float16, jnp.bfloat16
MIB = 1024 * 1024
GROUP = 6
SCALAR = pl.BlockSpec(memory_space=pltpu.SMEM)


def unrotate_kernel(peers, cos_ref, sin_ref, *refs):
    msgs, (unrot_ref, weighted_ref, gain_ref, rows_ref, rot_ref) = refs[:-5], refs[-5:]
    step = pl.program_id(0)
    parts = cos_ref.shape[0]
    per = parts // peers
    block = msgs[0].shape[1]

    @pl.when(step == 0)
    def _():
        for b, msg in enumerate(msgs):
            at = slice(b * block, (b + 1) * block)
            real_part, imag_part = msg[:parts].astype(F32), msg[parts : 2 * parts].astype(F32)
            cosine, sine = cos_ref[:, at], sin_ref[:, at]
            rows_ref[:parts, at] = (real_part * cosine + imag_part * sine).astype(BF16)
            rows_ref[parts : 2 * parts, at] = (imag_part * cosine - real_part * sine).astype(BF16)
            rows_ref[2 * parts :, at] = msg[2 * parts : 2 * parts + 16]
            code = msg[2 * parts + 16 :].astype(F32)
            goal = jnp.where(code > 0.0, code - 1.0, 255.0 - code)
            rot_ref[:, :, at] = goal.reshape(rot_ref.shape[0], 8, block)

    place = lax.broadcasted_iota(jnp.int32, (block, block), 1).astype(F32)
    gain_ref[...] = jnp.zeros_like(gain_ref)
    for b in range(len(msgs)):
        at = slice(b * block, (b + 1) * block)
        goal = rot_ref[step, :, at].T
        tables = [jnp.where(place == goal[:, i : i + 1], 1.0, 0.0).astype(BF16) for i in range(GROUP)]
        out = jnp.dot(rows_ref[:, at], jnp.concatenate(tables, axis=1), preferred_element_type=F32)
        turned = [out[:, i * block : (i + 1) * block] for i in range(GROUP)]
        gains = [jnp.sum(t[2 * parts :], axis=0, keepdims=True) for t in turned]
        for i in range(GROUP):
            gain_ref[0, i : i + 1, at] = gains[i]
        for c in range(2):
            plain, scaled = [], []
            for pair in range(0, GROUP, 2):
                for p in range(peers):
                    for i in (pair, pair + 1):
                        start = c * parts + p * per
                        piece = turned[i][start : start + per]
                        plain.append(piece)
                        scaled.append(piece * gains[i])
            unrot_ref[c, :, at] = jnp.concatenate(plain).astype(BF16)
            weighted_ref[c, :, at] = jnp.concatenate(scaled).astype(BF16)


def unrotate(cosine, sine, msgs, rots, peers):
    parts, pixels = cosine.shape
    steps = rots // GROUP
    spec = pl.BlockSpec((2, GROUP * parts, pixels), lambda r: (0, r, 0))
    shape = jax.ShapeDtypeStruct((2, rots * parts, pixels), BF16)
    whole = [pl.BlockSpec(a.shape, lambda r: (0, 0)) for a in (cosine, sine, *msgs)]
    return pl.pallas_call(
        functools.partial(unrotate_kernel, peers),
        grid=(steps,),
        in_specs=whole,
        out_specs=[spec, spec, pl.BlockSpec((1, 8, pixels), lambda r: (r, 0, 0))],
        out_shape=[shape, shape, jax.ShapeDtypeStruct((steps, 8, pixels), F32)],
        scratch_shapes=[pltpu.VMEM((2 * parts + 16, pixels), BF16), pltpu.VMEM((steps, 8, pixels), F32)],
        compiler_params=pltpu.CompilerParams(vmem_limit_bytes=56 * MIB),
        cost_estimate=pl.CostEstimate(
            flops=2 * rots * (2 * parts + 16) * pixels * msgs[0].shape[1],
            bytes_accessed=8 * rots * parts * pixels,
            transcendentals=0,
        ),
    )(cosine, sine, *msgs)


def score_kernel(peers, place_ref, weighted_ref, gain_ref, own_ref, other_ref, out_ref, refs_ref, norm_ref):
    step = pl.program_id(0)
    count, k2, block = own_ref.shape
    k_dev = k2 // 2
    blocks = refs_ref.shape[1] // block

    @pl.when(step == 0)
    def _():
        for b in range(blocks):
            at = slice(b * block, (b + 1) * block)
            power = 0.0
            for c in range(2):
                held = []
                for ref in (own_ref, other_ref):
                    for d in range(count // blocks):
                        held.append(ref[d * blocks + (place_ref[0] ^ b), c * k_dev : (c + 1) * k_dev])
                turned = jnp.concatenate(held).astype(F32).T
                refs_ref[c, at, :] = turned.astype(BF16)
                power = power + turned * turned
            gain = gain_ref[:, :, at].reshape(norm_ref.shape[0], block)
            part = 0.5 * jnp.dot(gain, power, preferred_element_type=F32, precision=lax.Precision.HIGHEST)
            norm_ref[...] = part if b == 0 else norm_ref[...] + part

    cross = jnp.dot(weighted_ref[0], refs_ref[0], preferred_element_type=F32)
    cross += jnp.dot(weighted_ref[1], refs_ref[1], preferred_element_type=F32)
    rows = cross.shape[0] // (GROUP * peers)
    norm = norm_ref[pl.ds(pl.multiple_of(step * 8, 8), 8), :]
    for q in range(GROUP // 2):
        for p in range(peers):
            for i in range(2):
                start = ((q * peers + p) * 2 + i) * rows
                to = (q * 2 + i) * rows
                out_ref[p, to : to + rows, :] = cross[start : start + rows] - norm[q * 2 + i : q * 2 + i + 1]


def score(place, weighted, gain, own, other, peers):
    steps, _, pixels = gain.shape
    count, k2, block = own.shape
    classes = count * k2 // (pixels // block)
    rows = weighted.shape[1] // steps
    return pl.pallas_call(
        functools.partial(score_kernel, peers),
        grid=(steps,),
        in_specs=[
            SCALAR,
            pl.BlockSpec((2, rows, pixels), lambda i: (0, i, 0)),
            pl.BlockSpec(gain.shape, lambda i: (0, 0, 0)),
            pl.BlockSpec(own.shape, lambda i: (0, 0, 0)),
            pl.BlockSpec(other.shape, lambda i: (0, 0, 0)),
        ],
        out_specs=pl.BlockSpec((peers, rows // peers, classes), lambda i: (0, i, 0)),
        out_shape=jax.ShapeDtypeStruct((peers, rows // peers * steps, classes), F32),
        scratch_shapes=[pltpu.VMEM((2, pixels, classes), BF16), pltpu.VMEM((steps * 8, classes), F32)],
        compiler_params=pltpu.CompilerParams(vmem_limit_bytes=56 * MIB),
    )(place, weighted, gain, own, other)


def sums_kernel(steps, block, k_dev, place_ref, weights_ref, unrot_ref, out_ref, acc_ref, totals_ref):
    step = pl.program_id(0)
    peers, mine, classes = weights_ref.shape
    picked = [weights_ref[p, q * 16 : (q + 1) * 16, :] for q in range(mine // 16) for p in range(peers)]
    turned = jnp.concatenate(picked).astype(F32).T.astype(BF16)
    count = jnp.dot(turned, jnp.ones((turned.shape[1], 128), BF16), preferred_element_type=F32)
    terms = [jnp.dot(turned, unrot_ref[c], preferred_element_type=F32) for c in range(2)]

    @pl.when(step == 0)
    def _():
        for c in range(2):
            acc_ref[c] = terms[c]
        totals_ref[...] = count

    @pl.when(step > 0)
    def _():
        for c in range(2):
            acc_ref[c] += terms[c]
        totals_ref[...] += count

    @pl.when(step == steps - 1)
    def _():
        blocks = acc_ref.shape[2] // block
        totals = totals_ref[...]
        high = totals.astype(BF16).astype(F32)
        lane = lax.broadcasted_iota(jnp.int32, totals.shape, 1)
        tail = jnp.where(lane == 0, high, totals - high)
        for d in range(classes // k_dev):
            ks = slice(d * k_dev, (d + 1) * k_dev)
            for b in range(blocks):
                at = d * blocks + (place_ref[0] ^ b)
                for c in range(2):
                    out_ref[at, :, c * block : (c + 1) * block] = acc_ref[c, ks, b * block : (b + 1) * block]
                out_ref[at, :, 2 * block :] = tail[ks]


def class_sums(place, weights, unrot, block, k_dev, side, steps):
    peers, total, classes = weights.shape
    pixels = unrot.shape[2]
    mine = total // steps
    half = classes // 2
    out = (half // k_dev * (pixels // block), k_dev, 2 * block + 128)
    return pl.pallas_call(
        functools.partial(sums_kernel, steps, block, k_dev),
        grid=(steps,),
        in_specs=[
            SCALAR,
            pl.BlockSpec((peers, mine, half), lambda i: (0, i, side)),
            pl.BlockSpec((2, mine * peers, pixels), lambda i: (0, i, 0)),
        ],
        out_specs=pl.BlockSpec(out, lambda i: (0, 0, 0)),
        out_shape=jax.ShapeDtypeStruct(out, F32),
        scratch_shapes=[pltpu.VMEM((2, half, pixels), F32), pltpu.VMEM((half, 128), F32)],
        compiler_params=pltpu.CompilerParams(vmem_limit_bytes=56 * MIB),
        cost_estimate=pl.CostEstimate(
            flops=4 * half * total * peers * pixels, bytes_accessed=unrot.size * 2, transcendentals=0
        ),
    )(place, weights, unrot)


def shards(particles, references, trans_index, shell_map, rot_index, inv_sigma):
    _, parts, freq = particles.shape
    k_dev = references.shape[0]
    rots = rot_index.shape[0]
    shells = inv_sigma.shape[0]
    cols, zqs = lax.axis_size("col"), lax.axis_size("zq")
    few = parts // 4
    classes = 2 * cols * k_dev
    yh, zq, zl = lax.axis_index("yh"), lax.axis_index("zq"), lax.axis_index("zl")
    half = 2 * zqs
    place = yh * 2 + zl

    base = (yh * half + zq * 2 + zl) * freq
    local_rot = rot_index - base
    code = jnp.where(local_rot < 256, local_rot + 1, 255 - local_rot).astype(BF16)
    code = jnp.pad(code.reshape(rots // GROUP, GROUP, freq), ((0, 0), (0, 8 - GROUP), (0, 0)))
    select = shell_map[:, None] == jnp.arange(shells, dtype=jnp.int32)[None, :]
    gain = jnp.sum(jnp.where(select, inv_sigma[None, :], 0.0), axis=1)
    top = lax.reduce_precision(gain, 8, 7)
    middle = lax.reduce_precision(gain - top, 8, 7)
    low = gain - top - middle
    gains = jnp.pad(jnp.stack([top, middle, low]).astype(BF16), ((0, 13), (0, 0)))
    side = jnp.concatenate([gains, code.reshape(rots // GROUP * 8, freq)])
    msgs = []
    for b in range(4):
        chunk = lax.dynamic_slice_in_dim(particles, (place ^ b) * few, few, 1).reshape(2 * few, freq)
        msg = jnp.concatenate([chunk, side])
        if b:
            msg = lax.ppermute(msg, ("yh", "zl"), [(i, i ^ b) for i in range(4)])
        msgs.append(msg)

    mine = references.transpose(1, 0, 2).reshape(1, 2 * k_dev, freq)
    mine = jnp.broadcast_to(mine, (4 * cols, 2 * k_dev, freq))
    refs = lax.all_to_all(mine, ("col", "yh", "zl"), 0, 0)

    pos = jnp.arange(freq, dtype=jnp.int32)
    spots = [place ^ b for b in range(4)]
    fidx = jnp.concatenate([(s // 2 * half + zq * 2 + s % 2) * freq + pos for s in spots])
    trans = lax.dynamic_slice_in_dim(trans_index, place * few, few, 0)
    kx = (fidx % 64).astype(F32)
    ky = (fidx // 64 % 128 - 64).astype(F32)
    tx = (trans % 7 - 3).astype(F32)
    ty = (trans // 7 - 3).astype(F32)
    phase = 2.0 * jnp.pi / 128.0 * (tx[:, None] * kx[None, :] + ty[:, None] * ky[None, :])
    unrot, weighted, gain_unrot = unrotate(jnp.cos(phase), jnp.sin(phase), msgs, rots, zqs)

    refs, weighted = lax.optimization_barrier((refs, weighted))
    refs_other = lax.ppermute(refs, "core", [(0, 1), (1, 0)])

    spot = jnp.reshape(place, (1,)).astype(jnp.int32)
    partial = score(spot, weighted, gain_unrot, refs, refs_other, zqs).astype(F16)
    own = few // zqs
    scores = jnp.sum(lax.all_to_all(partial, "zq", 0, 0).astype(F32), axis=0).reshape(rots, own, classes)
    peak = jnp.max(scores, axis=(0, 2), keepdims=True)
    expo = jnp.exp(scores - peak)
    weights = (expo / jnp.sum(expo, axis=(0, 2), keepdims=True)).astype(BF16)
    spread = jnp.broadcast_to(weights.reshape(1, rots * own, classes), (zqs, rots * own, classes))
    weights = lax.all_to_all(spread, "zq", 0, 0)

    other = class_sums(spot, weights, unrot, freq, k_dev, 1, 3).astype(F16)
    other = lax.ppermute(other, "core", [(0, 1), (1, 0)])
    message = class_sums(spot, weights, unrot, freq, k_dev, 0, 3)
    message = (message + other.astype(F32)).astype(F16)
    message = lax.all_to_all(message, ("col", "yh", "zl"), 0, 0)
    summed = jnp.sum(message.astype(F32), axis=0)
    counts = summed[:, 2 * freq] + summed[:, 2 * freq + 1]
    return (summed[:, : 2 * freq] / (counts + 1.0)[:, None]).reshape(k_dev, 2, freq)


def solution(mesh):
    doms, others = mesh.devices.shape
    grid = Mesh(mesh.devices.reshape(doms // 2, 2, 2, others // 4, 2), ("col", "core", "yh", "zq", "zl"))
    dom, across = ("col", "core"), ("yh", "zq", "zl")
    return jax.shard_map(
        shards,
        mesh=grid,
        in_specs=(
            P(None, dom, across),
            P(dom, None, across),
            P(dom),
            P(across),
            P(None, across),
            P(),
        ),
        out_specs=P(dom, None, across),
        check_vma=False,
    )
```

```python
import functools
import jax
import jax.numpy as jnp
from jax import lax
from jax.experimental import pallas as pl
from jax.experimental.pallas import tpu as pltpu
from jax.sharding import Mesh, PartitionSpec as P

F32, F16, BF16 = jnp.float32, jnp.float16, jnp.bfloat16
MIB = 1024 * 1024
GROUP = 6
SCALAR = pl.BlockSpec(memory_space=pltpu.SMEM)


def unrotate_kernel(peers, cos_ref, sin_ref, *refs):
    msgs, (unrot_ref, weighted_ref, gain_ref, rows_ref, rot_ref) = refs[:-5], refs[-5:]
    step = pl.program_id(0)
    parts = cos_ref.shape[0]
    per = parts // peers
    block = msgs[0].shape[1]

    @pl.when(step == 0)
    def _():
        for b, msg in enumerate(msgs):
            at = slice(b * block, (b + 1) * block)
            real_part, imag_part = msg[:parts].astype(F32), msg[parts : 2 * parts].astype(F32)
            cosine, sine = cos_ref[:, at], sin_ref[:, at]
            rows_ref[:parts, at] = (real_part * cosine + imag_part * sine).astype(BF16)
            rows_ref[parts : 2 * parts, at] = (imag_part * cosine - real_part * sine).astype(BF16)
            rows_ref[2 * parts :, at] = msg[2 * parts : 2 * parts + 16]
            code = msg[2 * parts + 16 :].astype(F32)
            goal = jnp.where(code > 0.0, code - 1.0, 255.0 - code)
            rot_ref[:, :, at] = goal.reshape(rot_ref.shape[0], 8, block)

    place = lax.broadcasted_iota(jnp.int32, (block, block), 1).astype(F32)
    gain_ref[...] = jnp.zeros_like(gain_ref)
    for b in range(len(msgs)):
        at = slice(b * block, (b + 1) * block)
        goal = rot_ref[step, :, at].T
        tables = [jnp.where(place == goal[:, i : i + 1], 1.0, 0.0).astype(BF16) for i in range(GROUP)]
        out = jnp.dot(rows_ref[:, at], jnp.concatenate(tables, axis=1), preferred_element_type=F32)
        turned = [out[:, i * block : (i + 1) * block] for i in range(GROUP)]
        gains = [jnp.sum(t[2 * parts :], axis=0, keepdims=True) for t in turned]
        for i in range(GROUP):
            gain_ref[0, i : i + 1, at] = gains[i]
        for c in range(2):
            plain, scaled = [], []
            for pair in range(0, GROUP, 2):
                for p in range(peers):
                    for i in (pair, pair + 1):
                        start = c * parts + p * per
                        piece = turned[i][start : start + per]
                        plain.append(piece)
                        scaled.append(piece * gains[i])
            unrot_ref[c, :, at] = jnp.concatenate(plain).astype(BF16)
            weighted_ref[c, :, at] = jnp.concatenate(scaled).astype(BF16)


def unrotate(cosine, sine, msgs, rots, peers):
    parts, pixels = cosine.shape
    steps = rots // GROUP
    spec = pl.BlockSpec((2, GROUP * parts, pixels), lambda r: (0, r, 0))
    shape = jax.ShapeDtypeStruct((2, rots * parts, pixels), BF16)
    whole = [pl.BlockSpec(a.shape, lambda r: (0, 0)) for a in (cosine, sine, *msgs)]
    return pl.pallas_call(
        functools.partial(unrotate_kernel, peers),
        grid=(steps,),
        in_specs=whole,
        out_specs=[spec, spec, pl.BlockSpec((1, 8, pixels), lambda r: (r, 0, 0))],
        out_shape=[shape, shape, jax.ShapeDtypeStruct((steps, 8, pixels), F32)],
        scratch_shapes=[pltpu.VMEM((2 * parts + 16, pixels), BF16), pltpu.VMEM((steps, 8, pixels), F32)],
        compiler_params=pltpu.CompilerParams(vmem_limit_bytes=56 * MIB),
        cost_estimate=pl.CostEstimate(
            flops=2 * rots * (2 * parts + 16) * pixels * msgs[0].shape[1],
            bytes_accessed=8 * rots * parts * pixels,
            transcendentals=0,
        ),
    )(cosine, sine, *msgs)


def score_kernel(peers, per_step, place_ref, weighted_ref, gain_ref, own_ref, other_ref, out_ref, refs_ref, norm_ref):
    step = pl.program_id(0)
    count, k2, block = own_ref.shape
    k_dev = k2 // 2
    blocks = refs_ref.shape[1] // block

    @pl.when(step == 0)
    def _():
        for b in range(blocks):
            at = slice(b * block, (b + 1) * block)
            power = 0.0
            for c in range(2):
                held = []
                for ref in (own_ref, other_ref):
                    for d in range(count // blocks):
                        held.append(ref[d * blocks + (place_ref[0] ^ b), c * k_dev : (c + 1) * k_dev])
                turned = jnp.concatenate(held).astype(F32).T
                refs_ref[c, at, :] = turned.astype(BF16)
                power = power + turned * turned
            gain = gain_ref[:, :, at].reshape(norm_ref.shape[0], block)
            part = 0.5 * jnp.dot(gain, power, preferred_element_type=F32, precision=lax.Precision.HIGHEST)
            norm_ref[...] = part if b == 0 else norm_ref[...] + part

    cross = jnp.dot(weighted_ref[0], refs_ref[0], preferred_element_type=F32)
    cross += jnp.dot(weighted_ref[1], refs_ref[1], preferred_element_type=F32)
    rows = cross.shape[0] // (per_step * GROUP * peers)
    for g in range(per_step):
        norm = norm_ref[pl.ds(pl.multiple_of((step * per_step + g) * 8, 8), 8), :]
        for q in range(GROUP // 2):
            for p in range(peers):
                for i in range(2):
                    start = (((g * (GROUP // 2) + q) * peers + p) * 2 + i) * rows
                    to = (g * GROUP + q * 2 + i) * rows
                    out_ref[p, to : to + rows, :] = cross[start : start + rows] - norm[q * 2 + i : q * 2 + i + 1]


def score(place, weighted, gain, own, other, peers, per_step):
    groups, _, pixels = gain.shape
    steps = groups // per_step
    count, k2, block = own.shape
    classes = count * k2 // (pixels // block)
    rows = weighted.shape[1] // steps
    return pl.pallas_call(
        functools.partial(score_kernel, peers, per_step),
        grid=(steps,),
        in_specs=[
            SCALAR,
            pl.BlockSpec((2, rows, pixels), lambda i: (0, i, 0)),
            pl.BlockSpec(gain.shape, lambda i: (0, 0, 0)),
            pl.BlockSpec(own.shape, lambda i: (0, 0, 0)),
            pl.BlockSpec(other.shape, lambda i: (0, 0, 0)),
        ],
        out_specs=pl.BlockSpec((peers, rows // peers, classes), lambda i: (0, i, 0)),
        out_shape=jax.ShapeDtypeStruct((peers, rows // peers * steps, classes), F32),
        scratch_shapes=[pltpu.VMEM((2, pixels, classes), BF16), pltpu.VMEM((groups * 8, classes), F32)],
        compiler_params=pltpu.CompilerParams(vmem_limit_bytes=54 * MIB),
    )(place, weighted, gain, own, other)


def sums_kernel(steps, block, k_dev, place_ref, weights_ref, unrot_ref, own_ref, other_ref, acc_ref, totals_ref):
    step = pl.program_id(0)
    peers, mine, classes = weights_ref.shape
    picked = [weights_ref[p, q * 16 : (q + 1) * 16, :] for q in range(mine // 16) for p in range(peers)]
    turned = jnp.concatenate(picked).astype(F32).T.astype(BF16)
    count = jnp.dot(turned, jnp.ones((turned.shape[1], 128), BF16), preferred_element_type=F32)
    terms = [jnp.dot(turned, unrot_ref[c], preferred_element_type=F32) for c in range(2)]

    @pl.when(step == 0)
    def _():
        for c in range(2):
            acc_ref[c] = terms[c]
        totals_ref[...] = count

    @pl.when(step > 0)
    def _():
        for c in range(2):
            acc_ref[c] += terms[c]
        totals_ref[...] += count

    @pl.when(step == steps - 1)
    def _():
        blocks = acc_ref.shape[2] // block
        totals = totals_ref[...]
        high = totals.astype(BF16).astype(F32)
        lane = lax.broadcasted_iota(jnp.int32, totals.shape, 1)
        tail = jnp.where(lane == 0, high, totals - high)
        cols = classes // k_dev // 2
        for d in range(2 * cols):
            ks = slice(d * k_dev, (d + 1) * k_dev)
            out_ref = own_ref if d < cols else other_ref
            for b in range(blocks):
                at = d % cols * blocks + (place_ref[0] ^ b)
                for c in range(2):
                    out_ref[at, :, c * block : (c + 1) * block] = acc_ref[c, ks, b * block : (b + 1) * block]
                out_ref[at, :, 2 * block :] = tail[ks]


def class_sums(place, weights, unrot, block, k_dev, steps):
    peers, total, classes = weights.shape
    pixels = unrot.shape[2]
    mine = total // steps
    half = classes // 2
    out = (half // k_dev * (pixels // block), k_dev, 2 * block + 128)
    return pl.pallas_call(
        functools.partial(sums_kernel, steps, block, k_dev),
        grid=(steps,),
        in_specs=[
            SCALAR,
            pl.BlockSpec((peers, mine, classes), lambda i: (0, i, 0)),
            pl.BlockSpec((2, mine * peers, pixels), lambda i: (0, i, 0)),
        ],
        out_specs=[pl.BlockSpec(out, lambda i: (0, 0, 0))] * 2,
        out_shape=[jax.ShapeDtypeStruct(out, F32)] * 2,
        scratch_shapes=[pltpu.VMEM((2, classes, pixels), F32), pltpu.VMEM((classes, 128), F32)],
        compiler_params=pltpu.CompilerParams(vmem_limit_bytes=40 * MIB),
        cost_estimate=pl.CostEstimate(
            flops=4 * classes * total * peers * pixels, bytes_accessed=unrot.size * 2, transcendentals=0
        ),
    )(place, weights, unrot)


def shards(particles, references, trans_index, shell_map, rot_index, inv_sigma):
    _, parts, freq = particles.shape
    k_dev = references.shape[0]
    rots = rot_index.shape[0]
    shells = inv_sigma.shape[0]
    cols, zqs = lax.axis_size("col"), lax.axis_size("zq")
    few = parts // 4
    classes = 2 * cols * k_dev
    yh, zq, zl = lax.axis_index("yh"), lax.axis_index("zq"), lax.axis_index("zl")
    half = 2 * zqs
    place = yh * 2 + zl

    base = (yh * half + zq * 2 + zl) * freq
    local_rot = rot_index - base
    code = jnp.where(local_rot < 256, local_rot + 1, 255 - local_rot).astype(BF16)
    code = jnp.pad(code.reshape(rots // GROUP, GROUP, freq), ((0, 0), (0, 8 - GROUP), (0, 0)))
    select = shell_map[:, None] == jnp.arange(shells, dtype=jnp.int32)[None, :]
    gain = jnp.sum(jnp.where(select, inv_sigma[None, :], 0.0), axis=1)
    top = lax.reduce_precision(gain, 8, 7)
    middle = lax.reduce_precision(gain - top, 8, 7)
    low = gain - top - middle
    gains = jnp.pad(jnp.stack([top, middle, low]).astype(BF16), ((0, 13), (0, 0)))
    side = jnp.concatenate([gains, code.reshape(rots // GROUP * 8, freq)])
    msgs = []
    for b in range(4):
        chunk = lax.dynamic_slice_in_dim(particles, (place ^ b) * few, few, 1).reshape(2 * few, freq)
        msg = jnp.concatenate([chunk, side])
        if b:
            msg = lax.ppermute(msg, ("yh", "zl"), [(i, i ^ b) for i in range(4)])
        msgs.append(msg)

    pos = jnp.arange(freq, dtype=jnp.int32)
    spots = [place ^ b for b in range(4)]
    fidx = jnp.concatenate([(s // 2 * half + zq * 2 + s % 2) * freq + pos for s in spots])
    trans = lax.dynamic_slice_in_dim(trans_index, place * few, few, 0)
    kx = (fidx % 64).astype(F32)
    ky = (fidx // 64 % 128 - 64).astype(F32)
    tx = (trans % 7 - 3).astype(F32)
    ty = (trans // 7 - 3).astype(F32)
    phase = 2.0 * jnp.pi / 128.0 * (tx[:, None] * kx[None, :] + ty[:, None] * ky[None, :])
    cosine, sine = jnp.cos(phase), jnp.sin(phase)

    mine = references.transpose(1, 0, 2).reshape(1, 2 * k_dev, freq)
    mine, msgs, cosine, sine = lax.optimization_barrier((mine, msgs, cosine, sine))
    mine = jnp.broadcast_to(mine, (4 * cols, 2 * k_dev, freq))
    refs = lax.all_to_all(mine, ("col", "yh", "zl"), 0, 0)

    unrot, weighted, gain_unrot = unrotate(cosine, sine, msgs, rots, zqs)

    refs, weighted = lax.optimization_barrier((refs, weighted))
    refs_other = lax.ppermute(refs, "core", [(0, 1), (1, 0)])

    spot = jnp.reshape(place, (1,)).astype(jnp.int32)
    partial = score(spot, weighted, gain_unrot, refs, refs_other, zqs, 2).astype(F16)
    own = few // zqs
    scores = jnp.sum(lax.all_to_all(partial, "zq", 0, 0).astype(F32), axis=0).reshape(rots, own, classes)
    peak = jnp.max(scores, axis=(0, 2), keepdims=True)
    expo = jnp.exp(scores - peak)
    weights = (expo / jnp.sum(expo, axis=(0, 2), keepdims=True)).astype(BF16)
    spread = jnp.broadcast_to(weights.reshape(1, rots * own, classes), (zqs, rots * own, classes))
    weights = lax.all_to_all(spread, "zq", 0, 0)

    message, other = class_sums(spot, weights, unrot, freq, k_dev, 3)
    other = lax.ppermute(other.astype(F16), "core", [(0, 1), (1, 0)])
    message = (message + other.astype(F32)).astype(F16)
    message = lax.all_to_all(message, ("col", "yh", "zl"), 0, 0)
    summed = jnp.sum(message.astype(F32), axis=0)
    counts = summed[:, 2 * freq] + summed[:, 2 * freq + 1]
    return (summed[:, : 2 * freq] / (counts + 1.0)[:, None]).reshape(k_dev, 2, freq)


def solution(mesh):
    doms, others = mesh.devices.shape
    grid = Mesh(mesh.devices.reshape(doms // 2, 2, 2, others // 4, 2), ("col", "core", "yh", "zq", "zl"))
    dom, across = ("col", "core"), ("yh", "zq", "zl")
    return jax.shard_map(
        shards,
        mesh=grid,
        in_specs=(
            P(None, dom, across),
            P(dom, None, across),
            P(dom),
            P(across),
            P(None, across),
            P(),
        ),
        out_specs=P(dom, None, across),
        check_vma=False,
    )
```

```python
import functools
import jax
import jax.numpy as jnp
from jax import lax
from jax.experimental import pallas as pl
from jax.experimental.pallas import tpu as pltpu
from jax.sharding import Mesh, PartitionSpec as P

F32, F16, BF16 = jnp.float32, jnp.float16, jnp.bfloat16
MIB = 1024 * 1024
GROUP = 6
SCALAR = pl.BlockSpec(memory_space=pltpu.SMEM)


def unrotate_kernel(peers, cos_ref, sin_ref, *refs):
    msgs, (unrot_ref, weighted_ref, gain_ref, rows_ref, rot_ref) = refs[:-5], refs[-5:]
    step = pl.program_id(0)
    parts = cos_ref.shape[0]
    per = parts // peers
    block = msgs[0].shape[1]

    @pl.when(step == 0)
    def _():
        for b, msg in enumerate(msgs):
            at = slice(b * block, (b + 1) * block)
            real_part, imag_part = msg[:parts].astype(F32), msg[parts : 2 * parts].astype(F32)
            cosine, sine = cos_ref[:, at], sin_ref[:, at]
            rows_ref[:parts, at] = (real_part * cosine + imag_part * sine).astype(BF16)
            rows_ref[parts : 2 * parts, at] = (imag_part * cosine - real_part * sine).astype(BF16)
            rows_ref[2 * parts :, at] = msg[2 * parts : 2 * parts + 16]
            code = msg[2 * parts + 16 :].astype(F32)
            goal = jnp.where(code > 0.0, code - 257.0, -1.0 - code)
            rot_ref[:, :, at] = goal.reshape(rot_ref.shape[0], 8, block)

    place = (lax.broadcasted_iota(jnp.int32, (block, block), 1).astype(F32) - 256.0).astype(BF16)
    one, zero = jnp.ones((), BF16), jnp.zeros((), BF16)
    gain_ref[...] = jnp.zeros_like(gain_ref)
    for b in range(len(msgs)):
        at = slice(b * block, (b + 1) * block)
        goal = rot_ref[step, :, at].T.astype(BF16)
        tables = [jnp.where(place == goal[:, i : i + 1], one, zero) for i in range(GROUP)]
        out = jnp.dot(rows_ref[:, at], jnp.concatenate(tables, axis=1), preferred_element_type=F32)
        turned = [out[:, i * block : (i + 1) * block] for i in range(GROUP)]
        gains = [jnp.sum(t[2 * parts :], axis=0, keepdims=True) for t in turned]
        for i in range(GROUP):
            gain_ref[0, i : i + 1, at] = gains[i]
        for c in range(2):
            plain, scaled = [], []
            for pair in range(0, GROUP, 2):
                for p in range(peers):
                    for i in (pair, pair + 1):
                        start = c * parts + p * per
                        piece = turned[i][start : start + per]
                        plain.append(piece)
                        scaled.append(piece * gains[i])
            unrot_ref[c, :, at] = jnp.concatenate(plain).astype(BF16)
            weighted_ref[c, :, at] = jnp.concatenate(scaled).astype(BF16)


def unrotate(cosine, sine, msgs, rots, peers):
    parts, pixels = cosine.shape
    steps = rots // GROUP
    spec = pl.BlockSpec((2, GROUP * parts, pixels), lambda r: (0, r, 0))
    shape = jax.ShapeDtypeStruct((2, rots * parts, pixels), BF16)
    whole = [pl.BlockSpec(a.shape, lambda r: (0, 0)) for a in (cosine, sine, *msgs)]
    return pl.pallas_call(
        functools.partial(unrotate_kernel, peers),
        grid=(steps,),
        in_specs=whole,
        out_specs=[spec, spec, pl.BlockSpec((1, 8, pixels), lambda r: (r, 0, 0))],
        out_shape=[shape, shape, jax.ShapeDtypeStruct((steps, 8, pixels), F32)],
        scratch_shapes=[pltpu.VMEM((2 * parts + 16, pixels), BF16), pltpu.VMEM((steps, 8, pixels), F32)],
        compiler_params=pltpu.CompilerParams(vmem_limit_bytes=56 * MIB),
        cost_estimate=pl.CostEstimate(
            flops=2 * rots * (2 * parts + 16) * pixels * msgs[0].shape[1],
            bytes_accessed=8 * rots * parts * pixels,
            transcendentals=0,
        ),
    )(cosine, sine, *msgs)


def score_kernel(peers, per_step, place_ref, w0_ref, w1_ref, w2_ref, w3_ref, gain_ref, own_ref, other_ref, out_ref, refs_ref, norm_ref):
    step = pl.program_id(0)
    count, k2, block = own_ref.shape
    k_dev = k2 // 2
    blocks = refs_ref.shape[1] // block

    @pl.when(step == 0)
    def _():
        for b in range(blocks):
            at = slice(b * block, (b + 1) * block)
            power = 0.0
            for c in range(2):
                held = []
                for ref in (own_ref, other_ref):
                    for d in range(count // blocks):
                        held.append(ref[d * blocks + (place_ref[0] ^ b), c * k_dev : (c + 1) * k_dev])
                turned = jnp.concatenate(held).astype(F32).T
                refs_ref[c, at, :] = turned.astype(BF16)
                power = power + turned * turned
            gain = gain_ref[:, :, at].reshape(norm_ref.shape[0], block)
            part = 0.5 * jnp.dot(gain, power, preferred_element_type=F32, precision=lax.Precision.HIGHEST)
            norm_ref[...] = part if b == 0 else norm_ref[...] + part

    cross = 0.0
    for j, ref in enumerate((w0_ref, w1_ref, w2_ref, w3_ref)):
        width = ref.shape[2]
        held = refs_ref[j // 2, j % 2 * width : (j % 2 + 1) * width, :]
        cross += jnp.dot(ref[0], held, preferred_element_type=F32)
    rows = cross.shape[0] // (per_step * GROUP * peers)
    for g in range(per_step):
        norm = norm_ref[pl.ds(pl.multiple_of((step * per_step + g) * 8, 8), 8), :]
        for q in range(GROUP // 2):
            for p in range(peers):
                for i in range(2):
                    start = (((g * (GROUP // 2) + q) * peers + p) * 2 + i) * rows
                    to = (g * GROUP + q * 2 + i) * rows
                    out_ref[p, to : to + rows, :] = cross[start : start + rows] - norm[q * 2 + i : q * 2 + i + 1]


def streams(rows, pixels):
    return [
        pl.BlockSpec((1, rows, pixels // 2), functools.partial(lambda c, h, i: (c, i, h), c, h))
        for c in range(2)
        for h in range(2)
    ]


def score(place, weighted, gain, own, other, peers, per_step):
    groups, _, pixels = gain.shape
    steps = groups // per_step
    count, k2, block = own.shape
    classes = count * k2 // (pixels // block)
    rows = weighted.shape[1] // steps
    return pl.pallas_call(
        functools.partial(score_kernel, peers, per_step),
        grid=(steps,),
        in_specs=[
            SCALAR,
            *streams(rows, pixels),
            pl.BlockSpec(gain.shape, lambda i: (0, 0, 0)),
            pl.BlockSpec(own.shape, lambda i: (0, 0, 0)),
            pl.BlockSpec(other.shape, lambda i: (0, 0, 0)),
        ],
        out_specs=pl.BlockSpec((peers, rows // peers, classes), lambda i: (0, i, 0)),
        out_shape=jax.ShapeDtypeStruct((peers, rows // peers * steps, classes), F32),
        scratch_shapes=[pltpu.VMEM((2, pixels, classes), BF16), pltpu.VMEM((groups * 8, classes), F32)],
        compiler_params=pltpu.CompilerParams(vmem_limit_bytes=50 * MIB),
    )(place, *[weighted] * 4, gain, own, other)


def sums_kernel(steps, block, k_dev, place_ref, weights_ref, u0_ref, u1_ref, u2_ref, u3_ref, own_ref, other_ref, acc_ref, totals_ref):
    step = pl.program_id(0)
    peers, mine, classes = weights_ref.shape
    picked = [weights_ref[p, q * 16 : (q + 1) * 16, :] for q in range(mine // 16) for p in range(peers)]
    turned = jnp.concatenate(picked).astype(F32).T.astype(BF16)
    count = jnp.dot(turned, jnp.ones((turned.shape[1], 128), BF16), preferred_element_type=F32)

    @pl.when(step == 0)
    def _():
        acc_ref[...] = jnp.zeros_like(acc_ref)
        totals_ref[...] = jnp.zeros_like(totals_ref)

    totals_ref[...] += count
    for j, ref in enumerate((u0_ref, u1_ref, u2_ref, u3_ref)):
        width = ref.shape[2]
        acc_ref[j // 2, :, j % 2 * width : (j % 2 + 1) * width] += jnp.dot(turned, ref[0], preferred_element_type=F32)

    @pl.when(step == steps - 1)
    def _():
        blocks = acc_ref.shape[2] // block
        totals = totals_ref[...]
        high = totals.astype(BF16).astype(F32)
        lane = lax.broadcasted_iota(jnp.int32, totals.shape, 1)
        tail = jnp.where(lane == 0, high, totals - high)
        cols = classes // k_dev // 2
        for d in range(2 * cols):
            ks = slice(d * k_dev, (d + 1) * k_dev)
            out_ref = own_ref if d < cols else other_ref
            for b in range(blocks):
                at = d % cols * blocks + (place_ref[0] ^ b)
                for c in range(2):
                    out_ref[at, :, c * block : (c + 1) * block] = acc_ref[c, ks, b * block : (b + 1) * block]
                out_ref[at, :, 2 * block :] = tail[ks]


def class_sums(place, weights, unrot, block, k_dev, steps):
    peers, total, classes = weights.shape
    pixels = unrot.shape[2]
    mine = total // steps
    half = classes // 2
    out = (half // k_dev * (pixels // block), k_dev, 2 * block + 128)
    return pl.pallas_call(
        functools.partial(sums_kernel, steps, block, k_dev),
        grid=(steps,),
        in_specs=[
            SCALAR,
            pl.BlockSpec((peers, mine, classes), lambda i: (0, i, 0)),
            *streams(mine * peers, pixels),
        ],
        out_specs=[pl.BlockSpec(out, lambda i: (0, 0, 0))] * 2,
        out_shape=[jax.ShapeDtypeStruct(out, F32)] * 2,
        scratch_shapes=[pltpu.VMEM((2, classes, pixels), F32), pltpu.VMEM((classes, 128), F32)],
        compiler_params=pltpu.CompilerParams(vmem_limit_bytes=40 * MIB),
        cost_estimate=pl.CostEstimate(
            flops=4 * classes * total * peers * pixels, bytes_accessed=unrot.size * 2, transcendentals=0
        ),
    )(place, weights, *[unrot] * 4)


def shards(particles, references, trans_index, shell_map, rot_index, inv_sigma):
    _, parts, freq = particles.shape
    k_dev = references.shape[0]
    rots = rot_index.shape[0]
    shells = inv_sigma.shape[0]
    cols, zqs = lax.axis_size("col"), lax.axis_size("zq")
    few = parts // 4
    classes = 2 * cols * k_dev
    yh, zq, zl = lax.axis_index("yh"), lax.axis_index("zq"), lax.axis_index("zl")
    half = 2 * zqs
    place = yh * 2 + zl

    base = (yh * half + zq * 2 + zl) * freq
    local_rot = rot_index - base
    code = jnp.where(local_rot < 256, local_rot + 1, 255 - local_rot).astype(BF16)
    code = jnp.pad(code.reshape(rots // GROUP, GROUP, freq), ((0, 0), (0, 8 - GROUP), (0, 0)))
    select = shell_map[:, None] == jnp.arange(shells, dtype=jnp.int32)[None, :]
    gain = jnp.sum(jnp.where(select, inv_sigma[None, :], 0.0), axis=1)
    top = lax.reduce_precision(gain, 8, 7)
    middle = lax.reduce_precision(gain - top, 8, 7)
    low = gain - top - middle
    gains = jnp.pad(jnp.stack([top, middle, low]).astype(BF16), ((0, 13), (0, 0)))
    side = jnp.concatenate([gains, code.reshape(rots // GROUP * 8, freq)])
    msgs = []
    for b in range(4):
        chunk = lax.dynamic_slice_in_dim(particles, (place ^ b) * few, few, 1).reshape(2 * few, freq)
        msg = jnp.concatenate([chunk, side])
        if b:
            msg = lax.ppermute(msg, ("yh", "zl"), [(i, i ^ b) for i in range(4)])
        msgs.append(msg)

    pos = jnp.arange(freq, dtype=jnp.int32)
    spots = [place ^ b for b in range(4)]
    fidx = jnp.concatenate([(s // 2 * half + zq * 2 + s % 2) * freq + pos for s in spots])
    trans = lax.dynamic_slice_in_dim(trans_index, place * few, few, 0)
    kx = (fidx % 64).astype(F32)
    ky = (fidx // 64 % 128 - 64).astype(F32)
    tx = (trans % 7 - 3).astype(F32)
    ty = (trans // 7 - 3).astype(F32)
    phase = 2.0 * jnp.pi / 128.0 * (tx[:, None] * kx[None, :] + ty[:, None] * ky[None, :])
    cosine, sine = jnp.cos(phase), jnp.sin(phase)

    mine = references.transpose(1, 0, 2).reshape(1, 2 * k_dev, freq)
    mine = jnp.broadcast_to(mine, (4 * cols, 2 * k_dev, freq))
    mine, msgs, cosine, sine = lax.optimization_barrier((mine, msgs, cosine, sine))
    refs = lax.all_to_all(mine, ("col", "yh", "zl"), 0, 0)

    unrot, weighted, gain_unrot = unrotate(cosine, sine, msgs, rots, zqs)

    refs, weighted = lax.optimization_barrier((refs, weighted))
    refs_other = lax.ppermute(refs, "core", [(0, 1), (1, 0)])

    spot = jnp.reshape(place, (1,)).astype(jnp.int32)
    partial = score(spot, weighted, gain_unrot, refs, refs_other, zqs, 2).astype(F16)
    own = few // zqs
    scores = jnp.sum(lax.all_to_all(partial, "zq", 0, 0).astype(F32), axis=0).reshape(rots, own, classes)
    peak = jnp.max(scores, axis=(0, 2), keepdims=True)
    expo = jnp.exp(scores - peak)
    weights = (expo / jnp.sum(expo, axis=(0, 2), keepdims=True)).astype(BF16)
    spread = jnp.broadcast_to(weights.reshape(1, rots * own, classes), (zqs, rots * own, classes))
    weights = lax.all_to_all(spread, "zq", 0, 0)

    message, other = class_sums(spot, weights, unrot, freq, k_dev, 3)
    other = lax.ppermute(other.astype(F16), "core", [(0, 1), (1, 0)])
    message = (message + other.astype(F32)).astype(F16)
    message = lax.all_to_all(message, ("col", "yh", "zl"), 0, 0)
    summed = jnp.sum(message.astype(F32), axis=0)
    counts = summed[:, 2 * freq] + summed[:, 2 * freq + 1]
    return (summed[:, : 2 * freq] / (counts + 1.0)[:, None]).reshape(k_dev, 2, freq)


def solution(mesh):
    doms, others = mesh.devices.shape
    grid = Mesh(mesh.devices.reshape(doms // 2, 2, 2, others // 4, 2), ("col", "core", "yh", "zq", "zl"))
    dom, across = ("col", "core"), ("yh", "zq", "zl")
    return jax.shard_map(
        shards,
        mesh=grid,
        in_specs=(
            P(None, dom, across),
            P(dom, None, across),
            P(dom),
            P(across),
            P(None, across),
            P(),
        ),
        out_specs=P(dom, None, across),
        check_vma=False,
    )
```

```python
import functools
import jax
import jax.numpy as jnp
from jax import lax
from jax.experimental import pallas as pl
from jax.experimental.pallas import tpu as pltpu
from jax.sharding import Mesh, PartitionSpec as P

F32, F16, BF16 = jnp.float32, jnp.float16, jnp.bfloat16
MIB = 1024 * 1024
GROUP = 6
SCALAR = pl.BlockSpec(memory_space=pltpu.SMEM)


def prepare_kernel(spot_ref, sigma_ref, particles_ref, rot_ref, shell_ref, mine_ref, *refs):
    msgs, spread_ref = refs[:-1], refs[-1]
    few, freq = particles_ref.shape[1] // 4, rot_ref.shape[1]
    shell = shell_ref[...]
    gain = jnp.zeros((1, freq), F32)
    for s in range(sigma_ref.shape[0]):
        gain = jnp.where(shell == s, sigma_ref[s], gain)
    top = gain.astype(BF16).astype(F32)
    middle = (gain - top).astype(BF16).astype(F32)
    low = gain - top - middle
    gains = jnp.concatenate([top, middle, low, jnp.zeros((13, freq), F32)]).astype(BF16)
    local = rot_ref[...] - spot_ref[1]
    code = jnp.where(local < 256, local + 1, 255 - local).astype(F32)
    gap = jnp.zeros((8 - GROUP, freq), F32)
    rows = []
    for g in range(rot_ref.shape[0] // GROUP):
        rows += [code[g * GROUP : (g + 1) * GROUP], gap]
    code = jnp.concatenate(rows).astype(BF16)
    for b, msg in enumerate(msgs):
        start = pl.multiple_of((spot_ref[0] ^ b) * few, few)
        for c in range(2):
            msg[c * few : (c + 1) * few, :] = particles_ref[c, pl.ds(start, few), :]
        msg[2 * few : 2 * few + 16, :] = gains
        msg[2 * few + 16 :, :] = code
    for j in range(spread_ref.shape[0]):
        spread_ref[j] = mine_ref[...]


def prepare(spot, inv_sigma, particles, rot_index, shell_map, mine, count):
    _, parts, freq = particles.shape
    rows = parts // 2 + 16 + rot_index.shape[0] // GROUP * 8
    whole = pl.BlockSpec(memory_space=pltpu.VMEM)
    return pl.pallas_call(
        prepare_kernel,
        in_specs=[SCALAR, SCALAR, whole, whole, whole, whole],
        out_specs=[whole] * 5,
        out_shape=[jax.ShapeDtypeStruct((rows, freq), BF16)] * 4
        + [jax.ShapeDtypeStruct((count,) + mine.shape, BF16)],
        compiler_params=pltpu.CompilerParams(vmem_limit_bytes=16 * MIB),
    )(spot, inv_sigma, particles, rot_index, shell_map[None], mine)


def unrotate_kernel(peers, cos_ref, sin_ref, *refs):
    msgs, (unrot_ref, weighted_ref, gain_ref, rows_ref, rot_ref) = refs[:-5], refs[-5:]
    step = pl.program_id(0)
    parts = cos_ref.shape[0]
    per = parts // peers
    block = msgs[0].shape[1]

    @pl.when(step == 0)
    def _():
        for b, msg in enumerate(msgs):
            at = slice(b * block, (b + 1) * block)
            real_part, imag_part = msg[:parts].astype(F32), msg[parts : 2 * parts].astype(F32)
            cosine, sine = cos_ref[:, at], sin_ref[:, at]
            rows_ref[:parts, at] = (real_part * cosine + imag_part * sine).astype(BF16)
            rows_ref[parts : 2 * parts, at] = (imag_part * cosine - real_part * sine).astype(BF16)
            rows_ref[2 * parts :, at] = msg[2 * parts : 2 * parts + 16]
            code = msg[2 * parts + 16 :].astype(F32)
            goal = jnp.where(code > 0.0, code - 257.0, -1.0 - code)
            rot_ref[:, :, at] = goal.reshape(rot_ref.shape[0], 8, block)

    place = (lax.broadcasted_iota(jnp.int32, (block, block), 1).astype(F32) - 256.0).astype(BF16)
    one, zero = jnp.ones((), BF16), jnp.zeros((), BF16)
    gain_ref[...] = jnp.zeros_like(gain_ref)
    for b in range(len(msgs)):
        at = slice(b * block, (b + 1) * block)
        goal = rot_ref[step, :, at].T.astype(BF16)
        tables = [jnp.where(place == goal[:, i : i + 1], one, zero) for i in range(GROUP)]
        out = jnp.dot(rows_ref[:, at], jnp.concatenate(tables, axis=1), preferred_element_type=F32)
        turned = [out[:, i * block : (i + 1) * block] for i in range(GROUP)]
        gains = [jnp.sum(t[2 * parts :], axis=0, keepdims=True) for t in turned]
        for i in range(GROUP):
            gain_ref[0, i : i + 1, at] = gains[i]
        for c in range(2):
            plain, scaled = [], []
            for pair in range(0, GROUP, 2):
                for p in range(peers):
                    for i in (pair, pair + 1):
                        start = c * parts + p * per
                        piece = turned[i][start : start + per]
                        plain.append(piece)
                        scaled.append(piece * gains[i])
            unrot_ref[c, :, at] = jnp.concatenate(plain).astype(BF16)
            weighted_ref[c, :, at] = jnp.concatenate(scaled).astype(BF16)


def unrotate(cosine, sine, msgs, rots, peers):
    parts, pixels = cosine.shape
    steps = rots // GROUP
    spec = pl.BlockSpec((2, GROUP * parts, pixels), lambda r: (0, r, 0))
    shape = jax.ShapeDtypeStruct((2, rots * parts, pixels), BF16)
    whole = [pl.BlockSpec(a.shape, lambda r: (0, 0)) for a in (cosine, sine, *msgs)]
    return pl.pallas_call(
        functools.partial(unrotate_kernel, peers),
        grid=(steps,),
        in_specs=whole,
        out_specs=[spec, spec, pl.BlockSpec((1, 8, pixels), lambda r: (r, 0, 0))],
        out_shape=[shape, shape, jax.ShapeDtypeStruct((steps, 8, pixels), F32)],
        scratch_shapes=[pltpu.VMEM((2 * parts + 16, pixels), BF16), pltpu.VMEM((steps, 8, pixels), F32)],
        compiler_params=pltpu.CompilerParams(vmem_limit_bytes=56 * MIB),
        cost_estimate=pl.CostEstimate(
            flops=2 * rots * (2 * parts + 16) * pixels * msgs[0].shape[1],
            bytes_accessed=8 * rots * parts * pixels,
            transcendentals=0,
        ),
    )(cosine, sine, *msgs)


def score_kernel(peers, per_step, place_ref, w0_ref, w1_ref, w2_ref, w3_ref, gain_ref, own_ref, other_ref, out_ref, refs_ref, norm_ref):
    step = pl.program_id(0)
    count, k2, block = own_ref.shape
    k_dev = k2 // 2
    blocks = refs_ref.shape[1] // block

    @pl.when(step == 0)
    def _():
        for b in range(blocks):
            at = slice(b * block, (b + 1) * block)
            power = 0.0
            for c in range(2):
                held = []
                for ref in (own_ref, other_ref):
                    for d in range(count // blocks):
                        held.append(ref[d * blocks + (place_ref[0] ^ b), c * k_dev : (c + 1) * k_dev])
                turned = jnp.concatenate(held).astype(F32).T
                refs_ref[c, at, :] = turned.astype(BF16)
                power = power + turned * turned
            gain = gain_ref[:, :, at].reshape(norm_ref.shape[0], block)
            part = 0.5 * jnp.dot(gain, power, preferred_element_type=F32, precision=lax.Precision.HIGHEST)
            norm_ref[...] = part if b == 0 else norm_ref[...] + part

    cross = 0.0
    for j, ref in enumerate((w0_ref, w1_ref, w2_ref, w3_ref)):
        width = ref.shape[2]
        held = refs_ref[j // 2, j % 2 * width : (j % 2 + 1) * width, :]
        cross += jnp.dot(ref[0], held, preferred_element_type=F32)
    rows = cross.shape[0] // (per_step * GROUP * peers)
    for g in range(per_step):
        norm = norm_ref[pl.ds(pl.multiple_of((step * per_step + g) * 8, 8), 8), :]
        for q in range(GROUP // 2):
            for p in range(peers):
                for i in range(2):
                    start = (((g * (GROUP // 2) + q) * peers + p) * 2 + i) * rows
                    to = (g * GROUP + q * 2 + i) * rows
                    out_ref[p, to : to + rows, :] = cross[start : start + rows] - norm[q * 2 + i : q * 2 + i + 1]


def streams(rows, pixels):
    return [
        pl.BlockSpec((1, rows, pixels // 2), functools.partial(lambda c, h, i: (c, i, h), c, h))
        for c in range(2)
        for h in range(2)
    ]


def score(place, weighted, gain, own, other, peers, per_step):
    groups, _, pixels = gain.shape
    steps = groups // per_step
    count, k2, block = own.shape
    classes = count * k2 // (pixels // block)
    rows = weighted.shape[1] // steps
    return pl.pallas_call(
        functools.partial(score_kernel, peers, per_step),
        grid=(steps,),
        in_specs=[
            SCALAR,
            *streams(rows, pixels),
            pl.BlockSpec(gain.shape, lambda i: (0, 0, 0)),
            pl.BlockSpec(own.shape, lambda i: (0, 0, 0)),
            pl.BlockSpec(other.shape, lambda i: (0, 0, 0)),
        ],
        out_specs=pl.BlockSpec((peers, rows // peers, classes), lambda i: (0, i, 0)),
        out_shape=jax.ShapeDtypeStruct((peers, rows // peers * steps, classes), F32),
        scratch_shapes=[pltpu.VMEM((2, pixels, classes), BF16), pltpu.VMEM((groups * 8, classes), F32)],
        compiler_params=pltpu.CompilerParams(vmem_limit_bytes=50 * MIB),
    )(place, *[weighted] * 4, gain, own, other)


def sums_kernel(steps, block, k_dev, place_ref, weights_ref, u0_ref, u1_ref, u2_ref, u3_ref, own_ref, other_ref, acc_ref, totals_ref):
    step = pl.program_id(0)
    peers, mine, classes = weights_ref.shape
    picked = [weights_ref[p, q * 16 : (q + 1) * 16, :] for q in range(mine // 16) for p in range(peers)]
    turned = jnp.concatenate(picked).astype(F32).T.astype(BF16)
    count = jnp.dot(turned, jnp.ones((turned.shape[1], 128), BF16), preferred_element_type=F32)

    @pl.when(step == 0)
    def _():
        acc_ref[...] = jnp.zeros_like(acc_ref)
        totals_ref[...] = jnp.zeros_like(totals_ref)

    totals_ref[...] += count
    for j, ref in enumerate((u0_ref, u1_ref, u2_ref, u3_ref)):
        width = ref.shape[2]
        acc_ref[j // 2, :, j % 2 * width : (j % 2 + 1) * width] += jnp.dot(turned, ref[0], preferred_element_type=F32)

    @pl.when(step == steps - 1)
    def _():
        blocks = acc_ref.shape[2] // block
        totals = totals_ref[...]
        high = totals.astype(BF16).astype(F32)
        lane = lax.broadcasted_iota(jnp.int32, totals.shape, 1)
        tail = jnp.where(lane == 0, high, totals - high)
        cols = classes // k_dev // 2
        for d in range(2 * cols):
            ks = slice(d * k_dev, (d + 1) * k_dev)
            out_ref = own_ref if d < cols else other_ref
            for b in range(blocks):
                at = d % cols * blocks + (place_ref[0] ^ b)
                for c in range(2):
                    out_ref[at, :, c * block : (c + 1) * block] = acc_ref[c, ks, b * block : (b + 1) * block]
                out_ref[at, :, 2 * block :] = tail[ks]


def class_sums(place, weights, unrot, block, k_dev, steps):
    peers, total, classes = weights.shape
    pixels = unrot.shape[2]
    mine = total // steps
    half = classes // 2
    out = (half // k_dev * (pixels // block), k_dev, 2 * block + 128)
    return pl.pallas_call(
        functools.partial(sums_kernel, steps, block, k_dev),
        grid=(steps,),
        in_specs=[
            SCALAR,
            pl.BlockSpec((peers, mine, classes), lambda i: (0, i, 0)),
            *streams(mine * peers, pixels),
        ],
        out_specs=[pl.BlockSpec(out, lambda i: (0, 0, 0))] * 2,
        out_shape=[jax.ShapeDtypeStruct(out, F32)] * 2,
        scratch_shapes=[pltpu.VMEM((2, classes, pixels), F32), pltpu.VMEM((classes, 128), F32)],
        compiler_params=pltpu.CompilerParams(vmem_limit_bytes=40 * MIB),
        cost_estimate=pl.CostEstimate(
            flops=4 * classes * total * peers * pixels, bytes_accessed=unrot.size * 2, transcendentals=0
        ),
    )(place, weights, *[unrot] * 4)


def shards(particles, references, trans_index, shell_map, rot_index, inv_sigma):
    _, parts, freq = particles.shape
    k_dev = references.shape[0]
    rots = rot_index.shape[0]
    cols, zqs = lax.axis_size("col"), lax.axis_size("zq")
    few = parts // 4
    classes = 2 * cols * k_dev
    yh, zq, zl = lax.axis_index("yh"), lax.axis_index("zq"), lax.axis_index("zl")
    half = 2 * zqs
    place = yh * 2 + zl

    base = (yh * half + zq * 2 + zl) * freq
    spot = jnp.stack([place, base]).astype(jnp.int32)
    mine = references.transpose(1, 0, 2).reshape(2 * k_dev, freq)
    *msgs, mine = prepare(spot, inv_sigma, particles, rot_index, shell_map, mine, 4 * cols)
    for b in range(1, 4):
        msgs[b] = lax.ppermute(msgs[b], ("yh", "zl"), [(i, i ^ b) for i in range(4)])

    pos = jnp.arange(freq, dtype=jnp.int32)
    spots = [place ^ b for b in range(4)]
    fidx = jnp.concatenate([(s // 2 * half + zq * 2 + s % 2) * freq + pos for s in spots])
    trans = lax.dynamic_slice_in_dim(trans_index, place * few, few, 0)
    kx = (fidx % 64).astype(F32)
    ky = (fidx // 64 % 128 - 64).astype(F32)
    tx = (trans % 7 - 3).astype(F32)
    ty = (trans // 7 - 3).astype(F32)
    phase = 2.0 * jnp.pi / 128.0 * (tx[:, None] * kx[None, :] + ty[:, None] * ky[None, :])
    cosine, sine = jnp.cos(phase), jnp.sin(phase)

    mine, msgs, cosine, sine = lax.optimization_barrier((mine, msgs, cosine, sine))
    refs = lax.all_to_all(mine, ("col", "yh", "zl"), 0, 0)

    unrot, weighted, gain_unrot = unrotate(cosine, sine, msgs, rots, zqs)

    refs, weighted = lax.optimization_barrier((refs, weighted))
    refs_other = lax.ppermute(refs, "core", [(0, 1), (1, 0)])

    partial = score(spot, weighted, gain_unrot, refs, refs_other, zqs, 3).astype(F16)
    own = few // zqs
    scores = jnp.sum(lax.all_to_all(partial, "zq", 0, 0).astype(F32), axis=0).reshape(rots, own, classes)
    peak = jnp.max(scores, axis=(0, 2), keepdims=True)
    expo = jnp.exp(scores - peak)
    weights = (expo / jnp.sum(expo, axis=(0, 2), keepdims=True)).astype(BF16)
    spread = jnp.broadcast_to(weights.reshape(1, rots * own, classes), (zqs, rots * own, classes))
    weights = lax.all_to_all(spread, "zq", 0, 0)

    message, other = class_sums(spot, weights, unrot, freq, k_dev, 2)
    other = lax.ppermute(other.astype(F16), "core", [(0, 1), (1, 0)])
    message = (message + other.astype(F32)).astype(F16)
    message = lax.all_to_all(message, ("col", "yh", "zl"), 0, 0)
    summed = jnp.sum(message.astype(F32), axis=0)
    counts = summed[:, 2 * freq] + summed[:, 2 * freq + 1]
    return (summed[:, : 2 * freq] / (counts + 1.0)[:, None]).reshape(k_dev, 2, freq)


def solution(mesh):
    doms, others = mesh.devices.shape
    grid = Mesh(mesh.devices.reshape(doms // 2, 2, 2, others // 4, 2), ("col", "core", "yh", "zq", "zl"))
    dom, across = ("col", "core"), ("yh", "zq", "zl")
    return jax.shard_map(
        shards,
        mesh=grid,
        in_specs=(
            P(None, dom, across),
            P(dom, None, across),
            P(dom),
            P(across),
            P(None, across),
            P(),
        ),
        out_specs=P(dom, None, across),
        check_vma=False,
    )
```

```python
import functools
import jax
import jax.numpy as jnp
from jax import lax
from jax.experimental import pallas as pl
from jax.experimental.pallas import tpu as pltpu
from jax.sharding import Mesh, PartitionSpec as P

F32, F16, BF16 = jnp.float32, jnp.float16, jnp.bfloat16
MIB = 1024 * 1024
GROUP = 6
SCALAR = pl.BlockSpec(memory_space=pltpu.SMEM)


def prepare_kernel(spot_ref, sigma_ref, particles_ref, rot_ref, shell_ref, mine_ref, *refs):
    msgs, spread_ref = refs[:-1], refs[-1]
    few, freq = particles_ref.shape[1] // 4, rot_ref.shape[1]
    shell = shell_ref[...]
    gain = jnp.zeros((1, freq), F32)
    for s in range(sigma_ref.shape[0]):
        gain = jnp.where(shell == s, sigma_ref[s], gain)
    top = gain.astype(BF16).astype(F32)
    middle = (gain - top).astype(BF16).astype(F32)
    low = gain - top - middle
    gains = jnp.concatenate([top, middle, low, jnp.zeros((13, freq), F32)]).astype(BF16)
    local = rot_ref[...] - spot_ref[1]
    code = jnp.where(local < 256, local + 1, 255 - local).astype(F32)
    gap = jnp.zeros((8 - GROUP, freq), F32)
    rows = []
    for g in range(rot_ref.shape[0] // GROUP):
        rows += [code[g * GROUP : (g + 1) * GROUP], gap]
    code = jnp.concatenate(rows).astype(BF16)
    for b, msg in enumerate(msgs):
        start = pl.multiple_of((spot_ref[0] ^ b) * few, few)
        for c in range(2):
            msg[c * few : (c + 1) * few, :] = particles_ref[c, pl.ds(start, few), :]
        msg[2 * few : 2 * few + 16, :] = gains
        msg[2 * few + 16 :, :] = code
    for j in range(spread_ref.shape[0]):
        spread_ref[j] = mine_ref[...]


def prepare(spot, inv_sigma, particles, rot_index, shell_map, mine, count):
    _, parts, freq = particles.shape
    rows = parts // 2 + 16 + rot_index.shape[0] // GROUP * 8
    args = (particles, rot_index, shell_map[None], mine)
    outs = [(rows, freq)] * 4 + [(count,) + mine.shape]

    def block(shape):
        return pl.BlockSpec(shape, lambda i: (0,) * len(shape))

    return pl.pallas_call(
        prepare_kernel,
        grid=(1,),
        in_specs=[SCALAR, SCALAR] + [block(a.shape) for a in args],
        out_specs=[block(shape) for shape in outs],
        out_shape=[jax.ShapeDtypeStruct(shape, BF16) for shape in outs],
        compiler_params=pltpu.CompilerParams(vmem_limit_bytes=60 * MIB),
    )(spot, inv_sigma, *args)


def unrotate_kernel(peers, cos_ref, sin_ref, *refs):
    msgs, (unrot_ref, weighted_ref, gain_ref, rows_ref, rot_ref) = refs[:-5], refs[-5:]
    step = pl.program_id(0)
    parts = cos_ref.shape[0]
    per = parts // peers
    block = msgs[0].shape[1]

    @pl.when(step == 0)
    def _():
        for b, msg in enumerate(msgs):
            at = slice(b * block, (b + 1) * block)
            real_part, imag_part = msg[:parts].astype(F32), msg[parts : 2 * parts].astype(F32)
            cosine, sine = cos_ref[:, at], sin_ref[:, at]
            rows_ref[:parts, at] = (real_part * cosine + imag_part * sine).astype(BF16)
            rows_ref[parts : 2 * parts, at] = (imag_part * cosine - real_part * sine).astype(BF16)
            rows_ref[2 * parts :, at] = msg[2 * parts : 2 * parts + 16]
            code = msg[2 * parts + 16 :].astype(F32)
            goal = jnp.where(code > 0.0, code - 257.0, -1.0 - code)
            rot_ref[:, :, at] = goal.reshape(rot_ref.shape[0], 8, block)

    place = (lax.broadcasted_iota(jnp.int32, (block, block), 1).astype(F32) - 256.0).astype(BF16)
    one, zero = jnp.ones((), BF16), jnp.zeros((), BF16)
    gain_ref[...] = jnp.zeros_like(gain_ref)
    for b in range(len(msgs)):
        at = slice(b * block, (b + 1) * block)
        goal = rot_ref[step, :, at].T.astype(BF16)
        tables = [jnp.where(place == goal[:, i : i + 1], one, zero) for i in range(GROUP)]
        out = jnp.dot(rows_ref[:, at], jnp.concatenate(tables, axis=1), preferred_element_type=F32)
        turned = [out[:, i * block : (i + 1) * block] for i in range(GROUP)]
        gains = [jnp.sum(t[2 * parts :], axis=0, keepdims=True) for t in turned]
        for i in range(GROUP):
            gain_ref[0, i : i + 1, at] = gains[i]
        for c in range(2):
            plain, scaled = [], []
            for pair in range(0, GROUP, 2):
                for p in range(peers):
                    for i in (pair, pair + 1):
                        start = c * parts + p * per
                        piece = turned[i][start : start + per]
                        plain.append(piece)
                        scaled.append(piece * gains[i])
            unrot_ref[c, :, at] = jnp.concatenate(plain).astype(BF16)
            weighted_ref[c, :, at] = jnp.concatenate(scaled).astype(BF16)


def unrotate(cosine, sine, msgs, rots, peers):
    parts, pixels = cosine.shape
    steps = rots // GROUP
    spec = pl.BlockSpec((2, GROUP * parts, pixels), lambda r: (0, r, 0))
    shape = jax.ShapeDtypeStruct((2, rots * parts, pixels), BF16)
    whole = [pl.BlockSpec(a.shape, lambda r: (0, 0)) for a in (cosine, sine, *msgs)]
    return pl.pallas_call(
        functools.partial(unrotate_kernel, peers),
        grid=(steps,),
        in_specs=whole,
        out_specs=[spec, spec, pl.BlockSpec((1, 8, pixels), lambda r: (r, 0, 0))],
        out_shape=[shape, shape, jax.ShapeDtypeStruct((steps, 8, pixels), F32)],
        scratch_shapes=[pltpu.VMEM((2 * parts + 16, pixels), BF16), pltpu.VMEM((steps, 8, pixels), F32)],
        compiler_params=pltpu.CompilerParams(vmem_limit_bytes=56 * MIB),
        cost_estimate=pl.CostEstimate(
            flops=2 * rots * (2 * parts + 16) * pixels * msgs[0].shape[1],
            bytes_accessed=8 * rots * parts * pixels,
            transcendentals=0,
        ),
    )(cosine, sine, *msgs)


def score_kernel(peers, per_step, place_ref, w0_ref, w1_ref, w2_ref, w3_ref, gain_ref, own_ref, other_ref, out_ref, refs_ref, norm_ref):
    step = pl.program_id(0)
    count, k2, block = own_ref.shape
    k_dev = k2 // 2
    blocks = refs_ref.shape[1] // block

    @pl.when(step == 0)
    def _():
        for b in range(blocks):
            at = slice(b * block, (b + 1) * block)
            power = 0.0
            for c in range(2):
                held = []
                for ref in (own_ref, other_ref):
                    for d in range(count // blocks):
                        held.append(ref[d * blocks + (place_ref[0] ^ b), c * k_dev : (c + 1) * k_dev])
                turned = jnp.concatenate(held).astype(F32).T
                refs_ref[c, at, :] = turned.astype(BF16)
                power = power + turned * turned
            gain = gain_ref[:, :, at].reshape(norm_ref.shape[0], block)
            part = 0.5 * jnp.dot(gain, power, preferred_element_type=F32, precision=lax.Precision.HIGHEST)
            norm_ref[...] = part if b == 0 else norm_ref[...] + part

    cross = 0.0
    for j, ref in enumerate((w0_ref, w1_ref, w2_ref, w3_ref)):
        width = ref.shape[2]
        held = refs_ref[j // 2, j % 2 * width : (j % 2 + 1) * width, :]
        cross += jnp.dot(ref[0], held, preferred_element_type=F32)
    rows = cross.shape[0] // (per_step * GROUP * peers)
    for g in range(per_step):
        norm = norm_ref[pl.ds(pl.multiple_of((step * per_step + g) * 8, 8), 8), :]
        for q in range(GROUP // 2):
            for p in range(peers):
                for i in range(2):
                    start = (((g * (GROUP // 2) + q) * peers + p) * 2 + i) * rows
                    to = (g * GROUP + q * 2 + i) * rows
                    out_ref[p, to : to + rows, :] = cross[start : start + rows] - norm[q * 2 + i : q * 2 + i + 1]


def streams(rows, pixels):
    return [
        pl.BlockSpec((1, rows, pixels // 2), functools.partial(lambda c, h, i: (c, i, h), c, h))
        for c in range(2)
        for h in range(2)
    ]


def score(place, weighted, gain, own, other, peers, per_step):
    groups, _, pixels = gain.shape
    steps = groups // per_step
    count, k2, block = own.shape
    classes = count * k2 // (pixels // block)
    rows = weighted.shape[1] // steps
    return pl.pallas_call(
        functools.partial(score_kernel, peers, per_step),
        grid=(steps,),
        in_specs=[
            SCALAR,
            *streams(rows, pixels),
            pl.BlockSpec(gain.shape, lambda i: (0, 0, 0)),
            pl.BlockSpec(own.shape, lambda i: (0, 0, 0)),
            pl.BlockSpec(other.shape, lambda i: (0, 0, 0)),
        ],
        out_specs=pl.BlockSpec((peers, rows // peers, classes), lambda i: (0, i, 0)),
        out_shape=jax.ShapeDtypeStruct((peers, rows // peers * steps, classes), F32),
        scratch_shapes=[pltpu.VMEM((2, pixels, classes), BF16), pltpu.VMEM((groups * 8, classes), F32)],
        compiler_params=pltpu.CompilerParams(vmem_limit_bytes=50 * MIB),
    )(place, *[weighted] * 4, gain, own, other)


def sums_kernel(steps, block, k_dev, place_ref, weights_ref, u0_ref, u1_ref, u2_ref, u3_ref, own_ref, other_ref, acc_ref, totals_ref):
    step = pl.program_id(0)
    peers, mine, classes = weights_ref.shape
    picked = [weights_ref[p, q * 16 : (q + 1) * 16, :] for q in range(mine // 16) for p in range(peers)]
    turned = jnp.concatenate(picked).astype(F32).T.astype(BF16)
    count = jnp.dot(turned, jnp.ones((turned.shape[1], 128), BF16), preferred_element_type=F32)

    @pl.when(step == 0)
    def _():
        acc_ref[...] = jnp.zeros_like(acc_ref)
        totals_ref[...] = jnp.zeros_like(totals_ref)

    totals_ref[...] += count
    for j, ref in enumerate((u0_ref, u1_ref, u2_ref, u3_ref)):
        width = ref.shape[2]
        acc_ref[j // 2, :, j % 2 * width : (j % 2 + 1) * width] += jnp.dot(turned, ref[0], preferred_element_type=F32)

    @pl.when(step == steps - 1)
    def _():
        blocks = acc_ref.shape[2] // block
        totals = totals_ref[...]
        high = totals.astype(BF16).astype(F32)
        lane = lax.broadcasted_iota(jnp.int32, totals.shape, 1)
        tail = jnp.where(lane == 0, high, totals - high)
        cols = classes // k_dev // 2
        for d in range(2 * cols):
            ks = slice(d * k_dev, (d + 1) * k_dev)
            out_ref = own_ref if d < cols else other_ref
            for b in range(blocks):
                at = d % cols * blocks + (place_ref[0] ^ b)
                for c in range(2):
                    out_ref[at, :, c * block : (c + 1) * block] = acc_ref[c, ks, b * block : (b + 1) * block]
                out_ref[at, :, 2 * block :] = tail[ks]


def class_sums(place, weights, unrot, block, k_dev, steps):
    peers, total, classes = weights.shape
    pixels = unrot.shape[2]
    mine = total // steps
    half = classes // 2
    out = (half // k_dev * (pixels // block), k_dev, 2 * block + 128)
    return pl.pallas_call(
        functools.partial(sums_kernel, steps, block, k_dev),
        grid=(steps,),
        in_specs=[
            SCALAR,
            pl.BlockSpec((peers, mine, classes), lambda i: (0, i, 0)),
            *streams(mine * peers, pixels),
        ],
        out_specs=[pl.BlockSpec(out, lambda i: (0, 0, 0))] * 2,
        out_shape=[jax.ShapeDtypeStruct(out, F32)] * 2,
        scratch_shapes=[pltpu.VMEM((2, classes, pixels), F32), pltpu.VMEM((classes, 128), F32)],
        compiler_params=pltpu.CompilerParams(vmem_limit_bytes=40 * MIB),
        cost_estimate=pl.CostEstimate(
            flops=4 * classes * total * peers * pixels, bytes_accessed=unrot.size * 2, transcendentals=0
        ),
    )(place, weights, *[unrot] * 4)


def shards(particles, references, trans_index, shell_map, rot_index, inv_sigma):
    _, parts, freq = particles.shape
    k_dev = references.shape[0]
    rots = rot_index.shape[0]
    cols, zqs = lax.axis_size("col"), lax.axis_size("zq")
    few = parts // 4
    classes = 2 * cols * k_dev
    yh, zq, zl = lax.axis_index("yh"), lax.axis_index("zq"), lax.axis_index("zl")
    half = 2 * zqs
    place = yh * 2 + zl

    base = (yh * half + zq * 2 + zl) * freq
    spot = jnp.stack([place, base]).astype(jnp.int32)
    mine = references.transpose(1, 0, 2).reshape(2 * k_dev, freq)
    *msgs, mine = prepare(spot, inv_sigma, particles, rot_index, shell_map, mine, 4 * cols)
    for b in range(1, 4):
        msgs[b] = lax.ppermute(msgs[b], ("yh", "zl"), [(i, i ^ b) for i in range(4)])

    pos = jnp.arange(freq, dtype=jnp.int32)
    spots = [place ^ b for b in range(4)]
    fidx = jnp.concatenate([(s // 2 * half + zq * 2 + s % 2) * freq + pos for s in spots])
    trans = lax.dynamic_slice_in_dim(trans_index, place * few, few, 0)
    kx = (fidx % 64).astype(F32)
    ky = (fidx // 64 % 128 - 64).astype(F32)
    tx = (trans % 7 - 3).astype(F32)
    ty = (trans // 7 - 3).astype(F32)
    phase = 2.0 * jnp.pi / 128.0 * (tx[:, None] * kx[None, :] + ty[:, None] * ky[None, :])
    cosine, sine = jnp.cos(phase), jnp.sin(phase)

    mine, msgs, cosine, sine = lax.optimization_barrier((mine, msgs, cosine, sine))
    refs = lax.all_to_all(mine, ("col", "yh", "zl"), 0, 0)

    unrot, weighted, gain_unrot = unrotate(cosine, sine, msgs, rots, zqs)

    refs, weighted = lax.optimization_barrier((refs, weighted))
    refs_other = lax.ppermute(refs, "core", [(0, 1), (1, 0)])

    partial = score(spot, weighted, gain_unrot, refs, refs_other, zqs, 3).astype(F16)
    own = few // zqs
    scores = jnp.sum(lax.all_to_all(partial, "zq", 0, 0).astype(F32), axis=0).reshape(rots, own, classes)
    peak = jnp.max(scores, axis=(0, 2), keepdims=True)
    expo = jnp.exp(scores - peak)
    weights = (expo / jnp.sum(expo, axis=(0, 2), keepdims=True)).astype(BF16)
    spread = jnp.broadcast_to(weights.reshape(1, rots * own, classes), (zqs, rots * own, classes))
    weights = lax.all_to_all(spread, "zq", 0, 0)

    message, other = class_sums(spot, weights, unrot, freq, k_dev, 2)
    other = lax.ppermute(other.astype(F16), "core", [(0, 1), (1, 0)])
    message = (message + other.astype(F32)).astype(F16)
    message = lax.all_to_all(message, ("col", "yh", "zl"), 0, 0)
    summed = jnp.sum(message.astype(F32), axis=0)
    counts = summed[:, 2 * freq] + summed[:, 2 * freq + 1]
    return (summed[:, : 2 * freq] / (counts + 1.0)[:, None]).reshape(k_dev, 2, freq)


def solution(mesh):
    doms, others = mesh.devices.shape
    grid = Mesh(mesh.devices.reshape(doms // 2, 2, 2, others // 4, 2), ("col", "core", "yh", "zq", "zl"))
    dom, across = ("col", "core"), ("yh", "zq", "zl")
    return jax.shard_map(
        shards,
        mesh=grid,
        in_specs=(
            P(None, dom, across),
            P(dom, None, across),
            P(dom),
            P(across),
            P(None, across),
            P(),
        ),
        out_specs=P(dom, None, across),
        check_vma=False,
    )
```

```python
import functools
import jax
import jax.numpy as jnp
from jax import lax
from jax.experimental import pallas as pl
from jax.experimental.pallas import tpu as pltpu
from jax.sharding import Mesh, PartitionSpec as P

F32, F16, BF16 = jnp.float32, jnp.float16, jnp.bfloat16
MIB = 1024 * 1024
GROUP = 6
SCALAR = pl.BlockSpec(memory_space=pltpu.SMEM)


def prepare_kernel(sigma_ref, particles_ref, rot_ref, shell_ref, mine_ref, *refs):
    msgs, spread_ref = refs[:-1], refs[-1]
    few, freq = particles_ref.shape[1] // 4, rot_ref.shape[1]
    place = lax.axis_index("yh") * 2 + lax.axis_index("zl")
    zqs = lax.axis_size("zq")
    base = (lax.axis_index("yh") * 2 * zqs + lax.axis_index("zq") * 2 + lax.axis_index("zl")) * freq
    shell = shell_ref[...]
    gain = jnp.zeros((1, freq), F32)
    for s in range(sigma_ref.shape[0]):
        gain = jnp.where(shell == s, sigma_ref[s], gain)
    top = gain.astype(BF16).astype(F32)
    middle = (gain - top).astype(BF16).astype(F32)
    low = gain - top - middle
    gains = jnp.concatenate([top, middle, low, jnp.zeros((13, freq), F32)]).astype(BF16)
    local = rot_ref[...] - base
    code = jnp.where(local < 256, local + 1, 255 - local).astype(F32)
    gap = jnp.zeros((8 - GROUP, freq), F32)
    rows = []
    for g in range(rot_ref.shape[0] // GROUP):
        rows += [code[g * GROUP : (g + 1) * GROUP], gap]
    code = jnp.concatenate(rows).astype(BF16)
    for b, msg in enumerate(msgs):
        start = pl.multiple_of((place ^ b) * few, few)
        for c in range(2):
            msg[c * few : (c + 1) * few, :] = particles_ref[c, pl.ds(start, few), :]
        msg[2 * few : 2 * few + 16, :] = gains
        msg[2 * few + 16 :, :] = code
    mine = mine_ref[...].astype(F32)
    mine = jnp.concatenate([mine[:, c] for c in range(2)]).astype(BF16)
    for j in range(spread_ref.shape[0]):
        spread_ref[j] = mine


def prepare(inv_sigma, particles, rot_index, shell_map, references, count):
    _, parts, freq = particles.shape
    rows = parts // 2 + 16 + rot_index.shape[0] // GROUP * 8
    args = (particles, rot_index, shell_map[None], references)
    outs = [(rows, freq)] * 4 + [(count, references.shape[0] * 2, freq)]

    def block(shape):
        return pl.BlockSpec(shape, lambda i: (0,) * len(shape))

    return pl.pallas_call(
        prepare_kernel,
        grid=(1,),
        in_specs=[SCALAR] + [block(a.shape) for a in args],
        out_specs=[block(shape) for shape in outs],
        out_shape=[jax.ShapeDtypeStruct(shape, BF16) for shape in outs],
        compiler_params=pltpu.CompilerParams(vmem_limit_bytes=60 * MIB),
    )(inv_sigma, *args)


def unrotate_kernel(peers, cos_ref, sin_ref, *refs):
    msgs, (unrot_ref, weighted_ref, gain_ref, rows_ref, rot_ref) = refs[:-5], refs[-5:]
    step = pl.program_id(0)
    parts = cos_ref.shape[0]
    per = parts // peers
    block = msgs[0].shape[1]

    @pl.when(step == 0)
    def _():
        for b, msg in enumerate(msgs):
            at = slice(b * block, (b + 1) * block)
            real_part, imag_part = msg[:parts].astype(F32), msg[parts : 2 * parts].astype(F32)
            cosine, sine = cos_ref[:, at], sin_ref[:, at]
            rows_ref[:parts, at] = (real_part * cosine + imag_part * sine).astype(BF16)
            rows_ref[parts : 2 * parts, at] = (imag_part * cosine - real_part * sine).astype(BF16)
            rows_ref[2 * parts :, at] = msg[2 * parts : 2 * parts + 16]
            code = msg[2 * parts + 16 :].astype(F32)
            goal = jnp.where(code > 0.0, code - 257.0, -1.0 - code)
            rot_ref[:, :, at] = goal.reshape(rot_ref.shape[0], 8, block)

    place = (lax.broadcasted_iota(jnp.int32, (block, block), 1).astype(F32) - 256.0).astype(BF16)
    one, zero = jnp.ones((), BF16), jnp.zeros((), BF16)
    gain_ref[...] = jnp.zeros_like(gain_ref)
    for b in range(len(msgs)):
        at = slice(b * block, (b + 1) * block)
        goal = rot_ref[step, :, at].T.astype(BF16)
        tables = [jnp.where(place == goal[:, i : i + 1], one, zero) for i in range(GROUP)]
        out = jnp.dot(rows_ref[:, at], jnp.concatenate(tables, axis=1), preferred_element_type=F32)
        turned = [out[:, i * block : (i + 1) * block] for i in range(GROUP)]
        gains = [jnp.sum(t[2 * parts :], axis=0, keepdims=True) for t in turned]
        for i in range(GROUP):
            gain_ref[0, i : i + 1, at] = gains[i]
        for c in range(2):
            plain, scaled = [], []
            for pair in range(0, GROUP, 2):
                for p in range(peers):
                    for i in (pair, pair + 1):
                        start = c * parts + p * per
                        piece = turned[i][start : start + per]
                        plain.append(piece)
                        scaled.append(piece * gains[i])
            unrot_ref[c, :, at] = jnp.concatenate(plain).astype(BF16)
            weighted_ref[c, :, at] = jnp.concatenate(scaled).astype(BF16)


def unrotate(cosine, sine, msgs, rots, peers):
    parts, pixels = cosine.shape
    steps = rots // GROUP
    spec = pl.BlockSpec((2, GROUP * parts, pixels), lambda r: (0, r, 0))
    shape = jax.ShapeDtypeStruct((2, rots * parts, pixels), BF16)
    whole = [pl.BlockSpec(a.shape, lambda r: (0, 0)) for a in (cosine, sine, *msgs)]
    return pl.pallas_call(
        functools.partial(unrotate_kernel, peers),
        grid=(steps,),
        in_specs=whole,
        out_specs=[spec, spec, pl.BlockSpec((1, 8, pixels), lambda r: (r, 0, 0))],
        out_shape=[shape, shape, jax.ShapeDtypeStruct((steps, 8, pixels), F32)],
        scratch_shapes=[pltpu.VMEM((2 * parts + 16, pixels), BF16), pltpu.VMEM((steps, 8, pixels), F32)],
        compiler_params=pltpu.CompilerParams(vmem_limit_bytes=56 * MIB),
        cost_estimate=pl.CostEstimate(
            flops=2 * rots * (2 * parts + 16) * pixels * msgs[0].shape[1],
            bytes_accessed=8 * rots * parts * pixels,
            transcendentals=0,
        ),
    )(cosine, sine, *msgs)


def score_kernel(peers, per_step, place_ref, w0_ref, w1_ref, w2_ref, w3_ref, gain_ref, own_ref, other_ref, out_ref, refs_ref, norm_ref):
    step = pl.program_id(0)
    count, k2, block = own_ref.shape
    k_dev = k2 // 2
    blocks = refs_ref.shape[1] // block

    @pl.when(step == 0)
    def _():
        for b in range(blocks):
            at = slice(b * block, (b + 1) * block)
            power = 0.0
            for c in range(2):
                held = []
                for ref in (own_ref, other_ref):
                    for d in range(count // blocks):
                        held.append(ref[d * blocks + (place_ref[0] ^ b), c * k_dev : (c + 1) * k_dev])
                turned = jnp.concatenate(held).astype(F32).T
                refs_ref[c, at, :] = turned.astype(BF16)
                power = power + turned * turned
            gain = gain_ref[:, :, at].reshape(norm_ref.shape[0], block)
            part = 0.5 * jnp.dot(gain, power, preferred_element_type=F32, precision=lax.Precision.HIGHEST)
            norm_ref[...] = part if b == 0 else norm_ref[...] + part

    cross = 0.0
    for j, ref in enumerate((w0_ref, w1_ref, w2_ref, w3_ref)):
        width = ref.shape[2]
        held = refs_ref[j // 2, j % 2 * width : (j % 2 + 1) * width, :]
        cross += jnp.dot(ref[0], held, preferred_element_type=F32)
    rows = cross.shape[0] // (per_step * GROUP * peers)
    for g in range(per_step):
        norm = norm_ref[pl.ds(pl.multiple_of((step * per_step + g) * 8, 8), 8), :]
        for q in range(GROUP // 2):
            for p in range(peers):
                for i in range(2):
                    start = (((g * (GROUP // 2) + q) * peers + p) * 2 + i) * rows
                    to = (g * GROUP + q * 2 + i) * rows
                    out_ref[p, to : to + rows, :] = cross[start : start + rows] - norm[q * 2 + i : q * 2 + i + 1]


def streams(rows, pixels):
    return [
        pl.BlockSpec((1, rows, pixels // 2), functools.partial(lambda c, h, i: (c, i, h), c, h))
        for c in range(2)
        for h in range(2)
    ]


def score(place, weighted, gain, own, other, peers, per_step):
    groups, _, pixels = gain.shape
    steps = groups // per_step
    count, k2, block = own.shape
    classes = count * k2 // (pixels // block)
    rows = weighted.shape[1] // steps
    return pl.pallas_call(
        functools.partial(score_kernel, peers, per_step),
        grid=(steps,),
        in_specs=[
            SCALAR,
            *streams(rows, pixels),
            pl.BlockSpec(gain.shape, lambda i: (0, 0, 0)),
            pl.BlockSpec(own.shape, lambda i: (0, 0, 0)),
            pl.BlockSpec(other.shape, lambda i: (0, 0, 0)),
        ],
        out_specs=pl.BlockSpec((peers, rows // peers, classes), lambda i: (0, i, 0)),
        out_shape=jax.ShapeDtypeStruct((peers, rows // peers * steps, classes), F32),
        scratch_shapes=[pltpu.VMEM((2, pixels, classes), BF16), pltpu.VMEM((groups * 8, classes), F32)],
        compiler_params=pltpu.CompilerParams(vmem_limit_bytes=50 * MIB),
    )(place, *[weighted] * 4, gain, own, other)


def sums_kernel(steps, block, k_dev, place_ref, weights_ref, u0_ref, u1_ref, u2_ref, u3_ref, own_ref, other_ref, acc_ref, totals_ref):
    step = pl.program_id(0)
    peers, mine, classes = weights_ref.shape
    picked = [weights_ref[p, q * 16 : (q + 1) * 16, :] for q in range(mine // 16) for p in range(peers)]
    turned = jnp.concatenate(picked).astype(F32).T.astype(BF16)
    count = jnp.dot(turned, jnp.ones((turned.shape[1], 128), BF16), preferred_element_type=F32)

    @pl.when(step == 0)
    def _():
        acc_ref[...] = jnp.zeros_like(acc_ref)
        totals_ref[...] = jnp.zeros_like(totals_ref)

    totals_ref[...] += count
    for j, ref in enumerate((u0_ref, u1_ref, u2_ref, u3_ref)):
        width = ref.shape[2]
        acc_ref[j // 2, :, j % 2 * width : (j % 2 + 1) * width] += jnp.dot(turned, ref[0], preferred_element_type=F32)

    @pl.when(step == steps - 1)
    def _():
        blocks = acc_ref.shape[2] // block
        totals = totals_ref[...]
        high = totals.astype(BF16).astype(F32)
        lane = lax.broadcasted_iota(jnp.int32, totals.shape, 1)
        tail = jnp.where(lane == 0, high, totals - high)
        cols = classes // k_dev // 2
        for d in range(2 * cols):
            ks = slice(d * k_dev, (d + 1) * k_dev)
            out_ref = own_ref if d < cols else other_ref
            for b in range(blocks):
                at = d % cols * blocks + (place_ref[0] ^ b)
                for c in range(2):
                    out_ref[at, :, c * block : (c + 1) * block] = acc_ref[c, ks, b * block : (b + 1) * block]
                out_ref[at, :, 2 * block :] = tail[ks]


def class_sums(place, weights, unrot, block, k_dev, steps):
    peers, total, classes = weights.shape
    pixels = unrot.shape[2]
    mine = total // steps
    half = classes // 2
    out = (half // k_dev * (pixels // block), k_dev, 2 * block + 128)
    return pl.pallas_call(
        functools.partial(sums_kernel, steps, block, k_dev),
        grid=(steps,),
        in_specs=[
            SCALAR,
            pl.BlockSpec((peers, mine, classes), lambda i: (0, i, 0)),
            *streams(mine * peers, pixels),
        ],
        out_specs=[pl.BlockSpec(out, lambda i: (0, 0, 0))] * 2,
        out_shape=[jax.ShapeDtypeStruct(out, F32)] * 2,
        scratch_shapes=[pltpu.VMEM((2, classes, pixels), F32), pltpu.VMEM((classes, 128), F32)],
        compiler_params=pltpu.CompilerParams(vmem_limit_bytes=40 * MIB),
        cost_estimate=pl.CostEstimate(
            flops=4 * classes * total * peers * pixels, bytes_accessed=unrot.size * 2, transcendentals=0
        ),
    )(place, weights, *[unrot] * 4)


def shards(particles, references, trans_index, shell_map, rot_index, inv_sigma):
    _, parts, freq = particles.shape
    k_dev = references.shape[0]
    rots = rot_index.shape[0]
    cols, zqs = lax.axis_size("col"), lax.axis_size("zq")
    few = parts // 4
    classes = 2 * cols * k_dev
    yh, zq, zl = lax.axis_index("yh"), lax.axis_index("zq"), lax.axis_index("zl")
    half = 2 * zqs
    place = yh * 2 + zl

    *msgs, mine = prepare(inv_sigma, particles, rot_index, shell_map, references, 4 * cols)
    for b in range(1, 4):
        msgs[b] = lax.ppermute(msgs[b], ("yh", "zl"), [(i, i ^ b) for i in range(4)])

    pos = jnp.arange(freq, dtype=jnp.int32)
    spots = [place ^ b for b in range(4)]
    fidx = jnp.concatenate([(s // 2 * half + zq * 2 + s % 2) * freq + pos for s in spots])
    trans = lax.dynamic_slice_in_dim(trans_index, place * few, few, 0)
    kx = (fidx % 64).astype(F32)
    ky = (fidx // 64 % 128 - 64).astype(F32)
    tx = (trans % 7 - 3).astype(F32)
    ty = (trans // 7 - 3).astype(F32)
    phase = 2.0 * jnp.pi / 128.0 * (tx[:, None] * kx[None, :] + ty[:, None] * ky[None, :])
    cosine, sine = jnp.cos(phase), jnp.sin(phase)

    mine, msgs, cosine, sine = lax.optimization_barrier((mine, msgs, cosine, sine))
    refs = lax.all_to_all(mine, ("col", "yh", "zl"), 0, 0)

    unrot, weighted, gain_unrot = unrotate(cosine, sine, msgs, rots, zqs)

    refs, weighted = lax.optimization_barrier((refs, weighted))
    refs_other = lax.ppermute(refs, "core", [(0, 1), (1, 0)])

    spot = jnp.reshape(place, (1,)).astype(jnp.int32)
    partial = score(spot, weighted, gain_unrot, refs, refs_other, zqs, 3).astype(F16)
    own = few // zqs
    scores = jnp.sum(lax.all_to_all(partial, "zq", 0, 0).astype(F32), axis=0).reshape(rots, own, classes)
    peak = jnp.max(scores, axis=(0, 2), keepdims=True)
    expo = jnp.exp(scores - peak)
    weights = (expo / jnp.sum(expo, axis=(0, 2), keepdims=True)).astype(BF16)
    spread = jnp.broadcast_to(weights.reshape(1, rots * own, classes), (zqs, rots * own, classes))
    weights = lax.all_to_all(spread, "zq", 0, 0)

    message, other = class_sums(spot, weights, unrot, freq, k_dev, 2)
    other = lax.ppermute(other.astype(F16), "core", [(0, 1), (1, 0)])
    message = (message + other.astype(F32)).astype(F16)
    message = lax.all_to_all(message, ("col", "yh", "zl"), 0, 0)
    summed = jnp.sum(message.astype(F32), axis=0)
    counts = summed[:, 2 * freq] + summed[:, 2 * freq + 1]
    return (summed[:, : 2 * freq] / (counts + 1.0)[:, None]).reshape(k_dev, 2, freq)


def solution(mesh):
    doms, others = mesh.devices.shape
    grid = Mesh(mesh.devices.reshape(doms // 2, 2, 2, others // 4, 2), ("col", "core", "yh", "zq", "zl"))
    dom, across = ("col", "core"), ("yh", "zq", "zl")
    return jax.shard_map(
        shards,
        mesh=grid,
        in_specs=(
            P(None, dom, across),
            P(dom, None, across),
            P(dom),
            P(across),
            P(None, across),
            P(),
        ),
        out_specs=P(dom, None, across),
        check_vma=False,
    )
```

```python
import functools
import jax
import jax.numpy as jnp
from jax import lax
from jax.experimental import pallas as pl
from jax.experimental.pallas import tpu as pltpu
from jax.sharding import Mesh, PartitionSpec as P

F32, F16, BF16 = jnp.float32, jnp.float16, jnp.bfloat16
MIB = 1024 * 1024
GROUP = 6
SCALAR = pl.BlockSpec(memory_space=pltpu.SMEM)


def prepare_kernel(sigma_ref, particles_ref, rot_ref, shell_ref, mine_ref, *refs):
    msgs, spread_ref = refs[:-1], refs[-1]
    few, freq = particles_ref.shape[1] // 4, rot_ref.shape[1]
    place = lax.axis_index("yh") * 2 + lax.axis_index("zl")
    zqs = lax.axis_size("zq")
    base = (lax.axis_index("yh") * 2 * zqs + lax.axis_index("zq") * 2 + lax.axis_index("zl")) * freq
    shell = shell_ref[...]
    gain = jnp.zeros((1, freq), F32)
    for s in range(sigma_ref.shape[0]):
        gain = jnp.where(shell == s, sigma_ref[s], gain)
    top = gain.astype(BF16).astype(F32)
    middle = (gain - top).astype(BF16).astype(F32)
    low = gain - top - middle
    gains = jnp.concatenate([top, middle, low, jnp.zeros((13, freq), F32)]).astype(BF16)
    local = rot_ref[...] - base
    code = jnp.where(local < 256, local + 1, 255 - local).astype(F32)
    gap = jnp.zeros((8 - GROUP, freq), F32)
    rows = []
    for g in range(rot_ref.shape[0] // GROUP):
        rows += [code[g * GROUP : (g + 1) * GROUP], gap]
    code = jnp.concatenate(rows).astype(BF16)
    for b, msg in enumerate(msgs):
        start = pl.multiple_of((place ^ b) * few, few)
        for c in range(2):
            msg[c * few : (c + 1) * few, :] = particles_ref[c, pl.ds(start, few), :]
        msg[2 * few : 2 * few + 16, :] = gains
        msg[2 * few + 16 :, :] = code
    mine = mine_ref[...].astype(F32)
    mine = jnp.concatenate([mine[:, c] for c in range(2)]).astype(BF16)
    for j in range(spread_ref.shape[0]):
        spread_ref[j] = mine


def prepare(inv_sigma, particles, rot_index, shell_map, references, count):
    _, parts, freq = particles.shape
    rows = parts // 2 + 16 + rot_index.shape[0] // GROUP * 8
    args = (particles, rot_index, shell_map[None], references)
    outs = [(rows, freq)] * 4 + [(count, references.shape[0] * 2, freq)]

    def block(shape):
        return pl.BlockSpec(shape, lambda i: (0,) * len(shape))

    return pl.pallas_call(
        prepare_kernel,
        grid=(1,),
        in_specs=[SCALAR] + [block(a.shape) for a in args],
        out_specs=[block(shape) for shape in outs],
        out_shape=[jax.ShapeDtypeStruct(shape, BF16) for shape in outs],
        compiler_params=pltpu.CompilerParams(vmem_limit_bytes=60 * MIB),
    )(inv_sigma, *args)


def unrotate_kernel(peers, cos_ref, sin_ref, *refs):
    msgs, (unrot_ref, weighted_ref, gain_ref, rows_ref, rot_ref) = refs[:-5], refs[-5:]
    step = pl.program_id(0)
    parts = cos_ref.shape[0]
    per = parts // peers
    block = msgs[0].shape[1]

    @pl.when(step == 0)
    def _():
        for b, msg in enumerate(msgs):
            at = slice(b * block, (b + 1) * block)
            real_part, imag_part = msg[:parts].astype(F32), msg[parts : 2 * parts].astype(F32)
            cosine, sine = cos_ref[:, at], sin_ref[:, at]
            rows_ref[:parts, at] = (real_part * cosine + imag_part * sine).astype(BF16)
            rows_ref[parts : 2 * parts, at] = (imag_part * cosine - real_part * sine).astype(BF16)
            rows_ref[2 * parts :, at] = msg[2 * parts : 2 * parts + 16]
            code = msg[2 * parts + 16 :].astype(F32)
            goal = jnp.where(code > 0.0, code - 257.0, -1.0 - code)
            rot_ref[:, :, at] = goal.reshape(rot_ref.shape[0], 8, block)

    place = (lax.broadcasted_iota(jnp.int32, (block, block), 1).astype(F32) - 256.0).astype(BF16)
    one, zero = jnp.ones((), BF16), jnp.zeros((), BF16)
    gain_ref[...] = jnp.zeros_like(gain_ref)
    for b in range(len(msgs)):
        at = slice(b * block, (b + 1) * block)
        goal = rot_ref[step, :, at].T.astype(BF16)
        tables = [jnp.where(place == goal[:, i : i + 1], one, zero) for i in range(GROUP)]
        out = jnp.dot(rows_ref[:, at], jnp.concatenate(tables, axis=1), preferred_element_type=F32)
        turned = [out[:, i * block : (i + 1) * block] for i in range(GROUP)]
        gains = [jnp.sum(t[2 * parts :], axis=0, keepdims=True) for t in turned]
        for i in range(GROUP):
            gain_ref[0, i : i + 1, at] = gains[i]
        for c in range(2):
            plain, scaled = [], []
            for pair in range(0, GROUP, 2):
                for p in range(peers):
                    for i in (pair, pair + 1):
                        start = c * parts + p * per
                        piece = turned[i][start : start + per]
                        plain.append(piece)
                        scaled.append(piece * gains[i])
            unrot_ref[c, :, at] = jnp.concatenate(plain).astype(BF16)
            weighted_ref[c, :, at] = jnp.concatenate(scaled).astype(BF16)


def unrotate(cosine, sine, msgs, rots, peers):
    parts, pixels = cosine.shape
    steps = rots // GROUP
    spec = pl.BlockSpec((2, GROUP * parts, pixels), lambda r: (0, r, 0))
    shape = jax.ShapeDtypeStruct((2, rots * parts, pixels), BF16)
    whole = [pl.BlockSpec(a.shape, lambda r: (0, 0)) for a in (cosine, sine, *msgs)]
    return pl.pallas_call(
        functools.partial(unrotate_kernel, peers),
        grid=(steps,),
        in_specs=whole,
        out_specs=[spec, spec, pl.BlockSpec((1, 8, pixels), lambda r: (r, 0, 0))],
        out_shape=[shape, shape, jax.ShapeDtypeStruct((steps, 8, pixels), F32)],
        scratch_shapes=[pltpu.VMEM((2 * parts + 16, pixels), BF16), pltpu.VMEM((steps, 8, pixels), F32)],
        compiler_params=pltpu.CompilerParams(vmem_limit_bytes=56 * MIB),
        cost_estimate=pl.CostEstimate(
            flops=2 * rots * (2 * parts + 16) * pixels * msgs[0].shape[1],
            bytes_accessed=8 * rots * parts * pixels,
            transcendentals=0,
        ),
    )(cosine, sine, *msgs)


def score_kernel(peers, per_step, place_ref, w0_ref, w1_ref, w2_ref, w3_ref, gain_ref, own_ref, other_ref, out_ref, refs_ref, norm_ref):
    step = pl.program_id(0)
    count, k2, block = own_ref.shape
    k_dev = k2 // 2
    blocks = refs_ref.shape[1] // block

    @pl.when(step == 0)
    def _():
        for b in range(blocks):
            at = slice(b * block, (b + 1) * block)
            power = 0.0
            for c in range(2):
                held = []
                for ref in (own_ref, other_ref):
                    for d in range(count // blocks):
                        held.append(ref[d * blocks + (place_ref[0] ^ b), c * k_dev : (c + 1) * k_dev])
                turned = jnp.concatenate(held).astype(F32).T
                refs_ref[c, at, :] = turned.astype(BF16)
                power = power + turned * turned
            gain = gain_ref[:, :, at].reshape(norm_ref.shape[0], block)
            part = 0.5 * jnp.dot(gain, power, preferred_element_type=F32, precision=lax.Precision.HIGHEST)
            norm_ref[...] = part if b == 0 else norm_ref[...] + part

    cross = 0.0
    for j, ref in enumerate((w0_ref, w1_ref, w2_ref, w3_ref)):
        width = ref.shape[2]
        held = refs_ref[j // 2, j % 2 * width : (j % 2 + 1) * width, :]
        cross += jnp.dot(ref[0], held, preferred_element_type=F32)
    rows = cross.shape[0] // (per_step * GROUP * peers)
    for g in range(per_step):
        norm = norm_ref[pl.ds(pl.multiple_of((step * per_step + g) * 8, 8), 8), :]
        for q in range(GROUP // 2):
            for p in range(peers):
                for i in range(2):
                    start = (((g * (GROUP // 2) + q) * peers + p) * 2 + i) * rows
                    to = (g * GROUP + q * 2 + i) * rows
                    out_ref[p, to : to + rows, :] = cross[start : start + rows] - norm[q * 2 + i : q * 2 + i + 1]


def streams(rows, pixels):
    return [
        pl.BlockSpec((1, rows, pixels // 2), functools.partial(lambda c, h, i: (c, i, h), c, h))
        for c in range(2)
        for h in range(2)
    ]


def score(place, weighted, gain, own, other, peers, per_step):
    groups, _, pixels = gain.shape
    steps = groups // per_step
    count, k2, block = own.shape
    classes = count * k2 // (pixels // block)
    rows = weighted.shape[1] // steps
    return pl.pallas_call(
        functools.partial(score_kernel, peers, per_step),
        grid=(steps,),
        in_specs=[
            SCALAR,
            *streams(rows, pixels),
            pl.BlockSpec(gain.shape, lambda i: (0, 0, 0)),
            pl.BlockSpec(own.shape, lambda i: (0, 0, 0)),
            pl.BlockSpec(other.shape, lambda i: (0, 0, 0)),
        ],
        out_specs=pl.BlockSpec((peers, rows // peers, classes), lambda i: (0, i, 0)),
        out_shape=jax.ShapeDtypeStruct((peers, rows // peers * steps, classes), F32),
        scratch_shapes=[pltpu.VMEM((2, pixels, classes), BF16), pltpu.VMEM((groups * 8, classes), F32)],
        compiler_params=pltpu.CompilerParams(vmem_limit_bytes=50 * MIB),
    )(place, *[weighted] * 4, gain, own, other)


def sums_kernel(steps, block, k_dev, place_ref, weights_ref, u0_ref, u1_ref, u2_ref, u3_ref, own_ref, other_ref, acc_ref, totals_ref):
    step = pl.program_id(0)
    peers, mine, classes = weights_ref.shape
    picked = [weights_ref[p, q * 16 : (q + 1) * 16, :] for q in range(mine // 16) for p in range(peers)]
    turned = jnp.concatenate(picked).T
    count = jnp.dot(turned, jnp.ones((turned.shape[1], 128), BF16), preferred_element_type=F32)

    @pl.when(step == 0)
    def _():
        acc_ref[...] = jnp.zeros_like(acc_ref)
        totals_ref[...] = jnp.zeros_like(totals_ref)

    totals_ref[...] += count
    for j, ref in enumerate((u0_ref, u1_ref, u2_ref, u3_ref)):
        width = ref.shape[2]
        acc_ref[j // 2, :, j % 2 * width : (j % 2 + 1) * width] += jnp.dot(turned, ref[0], preferred_element_type=F32)

    @pl.when(step == steps - 1)
    def _():
        blocks = acc_ref.shape[2] // block
        totals = totals_ref[...]
        high = totals.astype(BF16).astype(F32)
        lane = lax.broadcasted_iota(jnp.int32, totals.shape, 1)
        tail = jnp.where(lane == 0, high, totals - high)
        cols = classes // k_dev // 2
        for d in range(2 * cols):
            ks = slice(d * k_dev, (d + 1) * k_dev)
            out_ref = own_ref if d < cols else other_ref
            for b in range(blocks):
                at = d % cols * blocks + (place_ref[0] ^ b)
                for c in range(2):
                    out_ref[at, :, c * block : (c + 1) * block] = acc_ref[c, ks, b * block : (b + 1) * block]
                out_ref[at, :, 2 * block :] = tail[ks]


def class_sums(place, weights, unrot, block, k_dev, steps):
    peers, total, classes = weights.shape
    pixels = unrot.shape[2]
    mine = total // steps
    half = classes // 2
    out = (half // k_dev * (pixels // block), k_dev, 2 * block + 128)
    return pl.pallas_call(
        functools.partial(sums_kernel, steps, block, k_dev),
        grid=(steps,),
        in_specs=[
            SCALAR,
            pl.BlockSpec((peers, mine, classes), lambda i: (0, i, 0)),
            *streams(mine * peers, pixels),
        ],
        out_specs=[pl.BlockSpec(out, lambda i: (0, 0, 0))] * 2,
        out_shape=[jax.ShapeDtypeStruct(out, F32)] * 2,
        scratch_shapes=[pltpu.VMEM((2, classes, pixels), F32), pltpu.VMEM((classes, 128), F32)],
        compiler_params=pltpu.CompilerParams(vmem_limit_bytes=40 * MIB),
        cost_estimate=pl.CostEstimate(
            flops=4 * classes * total * peers * pixels, bytes_accessed=unrot.size * 2, transcendentals=0
        ),
    )(place, weights, *[unrot] * 4)


def shards(particles, references, trans_index, shell_map, rot_index, inv_sigma):
    _, parts, freq = particles.shape
    k_dev = references.shape[0]
    rots = rot_index.shape[0]
    cols, zqs = lax.axis_size("col"), lax.axis_size("zq")
    few = parts // 4
    classes = 2 * cols * k_dev
    yh, zq, zl = lax.axis_index("yh"), lax.axis_index("zq"), lax.axis_index("zl")
    half = 2 * zqs
    place = yh * 2 + zl

    *msgs, mine = prepare(inv_sigma, particles, rot_index, shell_map, references, 4 * cols)
    for b in range(1, 4):
        msgs[b] = lax.ppermute(msgs[b], ("yh", "zl"), [(i, i ^ b) for i in range(4)])

    pos = jnp.arange(freq, dtype=jnp.int32)
    spots = [place ^ b for b in range(4)]
    fidx = jnp.concatenate([(s // 2 * half + zq * 2 + s % 2) * freq + pos for s in spots])
    trans = lax.dynamic_slice_in_dim(trans_index, place * few, few, 0)
    kx = (fidx % 64).astype(F32)
    ky = (fidx // 64 % 128 - 64).astype(F32)
    tx = (trans % 7 - 3).astype(F32)
    ty = (trans // 7 - 3).astype(F32)
    phase = 2.0 * jnp.pi / 128.0 * (tx[:, None] * kx[None, :] + ty[:, None] * ky[None, :])
    cosine, sine = jnp.cos(phase), jnp.sin(phase)

    mine, msgs, cosine, sine = lax.optimization_barrier((mine, msgs, cosine, sine))
    refs = lax.all_to_all(mine, ("col", "yh", "zl"), 0, 0)

    unrot, weighted, gain_unrot = unrotate(cosine, sine, msgs, rots, zqs)

    refs, weighted = lax.optimization_barrier((refs, weighted))
    refs_other = lax.ppermute(refs, "core", [(0, 1), (1, 0)])

    spot = jnp.reshape(place, (1,)).astype(jnp.int32)
    partial = score(spot, weighted, gain_unrot, refs, refs_other, zqs, 3).astype(F16)
    own = few // zqs
    scores = jnp.sum(lax.all_to_all(partial, "zq", 0, 0).astype(F32), axis=0).reshape(rots, own, classes)
    peak = jnp.max(scores, axis=(0, 2), keepdims=True)
    expo = jnp.exp(scores - peak)
    weights = (expo / jnp.sum(expo, axis=(0, 2), keepdims=True)).astype(BF16)
    spread = jnp.broadcast_to(weights.reshape(1, rots * own, classes), (zqs, rots * own, classes))
    weights = lax.all_to_all(spread, "zq", 0, 0)

    message, other = class_sums(spot, weights, unrot, freq, k_dev, 2)
    other = lax.ppermute(other.astype(F16), "core", [(0, 1), (1, 0)])
    message = (message + other.astype(F32)).astype(F16)
    message = lax.all_to_all(message, ("col", "yh", "zl"), 0, 0)
    summed = jnp.sum(message.astype(F32), axis=0)
    counts = summed[:, 2 * freq] + summed[:, 2 * freq + 1]
    return (summed[:, : 2 * freq] / (counts + 1.0)[:, None]).reshape(k_dev, 2, freq)


def solution(mesh):
    doms, others = mesh.devices.shape
    grid = Mesh(mesh.devices.reshape(doms // 2, 2, 2, others // 4, 2), ("col", "core", "yh", "zq", "zl"))
    dom, across = ("col", "core"), ("yh", "zq", "zl")
    return jax.shard_map(
        shards,
        mesh=grid,
        in_specs=(
            P(None, dom, across),
            P(dom, None, across),
            P(dom),
            P(across),
            P(None, across),
            P(),
        ),
        out_specs=P(dom, None, across),
        check_vma=False,
    )
```
